512 devices in a mesh: gx: 8 (over y), gy: 8 (over z), gz: 8 (over x, core).
Axes of the slice: x: 4, y: 8, z: 8, core: 2. Of those that a mesh axis runs over, the one named last changes fastest.
Arguments:
- coarse_density: float32 [64, 128, 512], P('gx', 'gy', 'gz'), may hold values from -6 to 6
- start_potential: float32 [128, 256, 1024], P('gx', 'gy', 'gz'), may hold values from -6 to 6
- pair_density: float32 [8192, 91], P(('gx', 'gy', 'gz')), may hold values from -6 to 6
- expansion: float32 [91, 9], replicated, may hold values from -0.625 to 0.625
- box_corners: int32 [8192, 3], P(('gx', 'gy', 'gz')), may hold values from 0 to 1023, as said below
- box_offsets: float32 [8192, 3], P(('gx', 'gy', 'gz')), may hold values from -0.5 to 0.5
- atom_lists: int32 [512, 44], P(('gx', 'gy', 'gz')), may hold values from 0 to 8191, as said below
- atom_counts: int32 [512], P(('gx', 'gy', 'gz')), may hold values from 16 to 44
Outputs:
- total_density: float32 [128, 256, 1024], P('gx', 'gy', 'gz')
- potential: float32 [128, 256, 1024], P('gx', 'gy', 'gz')
The draws below stay inside these ranges and needn't reach their ends.
Inputs may be any that keep to these rules, and one draw needn't show every extreme that they name: `box_corners`: atom dom * 16 + j belongs to domain dom. Its box of 12 cells along each dimension starts inside that domain; either it crosses the domain's three upper faces or it lies within the domain. `atom_lists`: row d lists, in no particular order, every atom whose box meets domain d: the domain's own 16 atoms and the crossing atoms of its lower neighbours along x, y, z and the diagonals; a domain has at most 4 crossing atoms. Entries past atom_counts[d] are 0.
All inputs are finite; a program needn't handle non-finite values.
Results may differ from the reference program's by a relative error of at most 0.0003.
Values sent between devices are 32-bit elements; how exact they have to be, the bound alone decides.
A program may use at most 128 MiB of HBM per device.

```python
import jax
import jax.numpy as jnp
from jax import lax

FX = 16
FY = 32
FZ = 128
A_DEV = 16
K_EDGE = 4
PAIRS = 91
LM = 9
BOX = 12
LEVELS = 5
CYCLES = 2
PRE = 1
POST = 1
COARSE_SWEEPS = 4
DOMAINS = 512
NX = 128
NY = 256
NZ = 1024
ATOMS = 8192
M_SLOTS = 44
N_GX = 8
N_GY = 8
N_GZ = 8


def atom_layout(key):
    count_x = NX // FX
    count_y = NY // FY
    count_z = NZ // FZ
    layout_key = jax.random.fold_in(key, 101)
    keys = jax.random.split(layout_key, 8)
    centre_x = jax.random.randint(keys[0], (), 1, count_x)
    centre_y = jax.random.randint(keys[1], (), 1, count_y)
    centre_z = jax.random.randint(keys[2], (), 1, count_z)
    index_x = jnp.arange(count_x, dtype=jnp.int32)[:, None, None]
    index_y = jnp.arange(count_y, dtype=jnp.int32)[None, :, None]
    index_z = jnp.arange(count_z, dtype=jnp.int32)[None, None, :]
    chosen = ((index_x == centre_x) | (index_x == centre_x - 1)) & ((index_y == centre_y) | (index_y == centre_y - 1)) & ((index_z == centre_z) | (index_z == centre_z - 1))
    topmost = (index_x == count_x - 1) & (index_y == count_y - 1) & (index_z == count_z - 1)
    drawn_edges = jax.random.randint(keys[3], (count_x, count_y, count_z), 0, K_EDGE + 1)
    edge_count = jnp.where(chosen | topmost, K_EDGE, drawn_edges)
    scores = jax.random.randint(keys[4], (count_x, count_y, count_z, A_DEV), 0, 1 << 16) * A_DEV + jnp.arange(A_DEV, dtype=jnp.int32)
    ranks = jnp.argsort(jnp.argsort(scores, axis=-1), axis=-1)
    edge = ranks < edge_count[..., None]
    forced = topmost[..., None] & (ranks == 0)
    columns = []
    for axis, extent, domain_index in ((0, FX, index_x), (1, FY, index_y), (2, FZ, index_z)):
        low = jnp.where(edge, extent - BOX + 1, 0)
        high = jnp.where(edge, extent, extent - BOX + 1)
        local = jax.random.randint(keys[5 + axis], edge.shape, low, high)
        local = jnp.where(forced, extent - 1, local)
        columns.append(local + domain_index[..., None] * extent)
    corners = jnp.stack(columns, axis=-1).reshape(ATOMS, 3).astype(jnp.int32)
    return (edge, corners)


def candidate_sets(edge):
    count_x, count_y, count_z = (edge.shape[0], edge.shape[1], edge.shape[2])
    base = jnp.arange(ATOMS, dtype=jnp.int32).reshape(count_x, count_y, count_z, A_DEV)
    id_parts = []
    valid_parts = []
    for off_z in (0, 1):
        for off_y in (0, 1):
            for off_x in (0, 1):
                widths = ((off_x, 0), (off_y, 0), (off_z, 0), (0, 0))
                if off_x + off_y + off_z == 0:
                    id_parts.append(base)
                    valid_parts.append(jnp.ones(edge.shape, dtype=bool))
                else:
                    id_parts.append(jnp.pad(base, widths)[:count_x, :count_y, :count_z])
                    valid_parts.append(jnp.pad(edge, widths)[:count_x, :count_y, :count_z])
    ids_all = jnp.concatenate(id_parts, axis=-1).reshape(DOMAINS, 8 * A_DEV)
    valid_all = jnp.concatenate(valid_parts, axis=-1).reshape(DOMAINS, 8 * A_DEV)
    return (ids_all, valid_all)


def draw_box_corners(key, part):
    edge, corners = atom_layout(key)
    return corners


def draw_atom_lists(key, part):
    edge, corners = atom_layout(key)
    ids_all, valid_all = candidate_sets(edge)
    key = jax.random.fold_in(key, 7)
    width = 8 * A_DEV
    position = jnp.arange(width, dtype=jnp.int32)
    scores = jax.random.randint(key, (DOMAINS, width), 0, 1 << 16) * width + position
    scores = jnp.where(valid_all, scores, (1 << 16) * width + position)
    order = jnp.argsort(scores, axis=1)[:, :M_SLOTS]
    taken_ids = jnp.take_along_axis(ids_all, order, axis=1)
    taken_valid = jnp.take_along_axis(valid_all, order, axis=1)
    return jnp.where(taken_valid, taken_ids, 0).astype(jnp.int32)


def draw_atom_counts(key, part):
    edge, corners = atom_layout(key)
    ids_all, valid_all = candidate_sets(edge)
    return jnp.sum(valid_all.astype(jnp.int32), axis=1).astype(jnp.int32)


def draw_coarse_density(key, part):
    key = jax.random.fold_in(key, 11)
    shape = (NX // 2, NY // 2, NZ // 2)
    return jnp.clip(jax.random.normal(key, shape, jnp.float32), -4.0, 4.0)


def level_of(rng, shape, pieces, low, high):
    def one(axis_at, blocks):
        draws = jax.random.uniform(jax.random.fold_in(jax.random.fold_in(rng, 6), axis_at), (blocks,), jnp.float32, low / len(pieces), high / len(pieces))
        return jnp.repeat(jnp.exp(draws), shape[axis_at] // blocks).reshape((-1,) + (1,) * (len(shape) - axis_at - 1))

    loudness = one(*pieces[0])
    for cut in pieces[1:]:
        loudness = loudness * one(*cut)
    return loudness


def bell_draw(rng, shape, scale, limit, shards=(), kind=jnp.bfloat16):
    entries = jax.random.normal(rng, shape, jnp.float32) * scale
    if len(shards) > 0:
        entries = level_of(rng, shape, shards, -0.22, 0.18) * entries
    return jnp.clip(entries, min=-limit, max=limit).astype(kind)


def setup_inputs(seed: int = 0) -> dict:
    splits = jax.random.split(jax.random.key(seed), 9)
    return {
        "coarse_density": draw_coarse_density(jax.random.fold_in(splits[8], 71), 0),
        "start_potential": bell_draw(splits[1], (NX, NY, NZ), 1.0, 6.0, ((0, 8), (1, 8), (2, 8)), jnp.float32),
        "pair_density": bell_draw(splits[2], (ATOMS, PAIRS), 1.0, 6.0, ((0, 512),), jnp.float32),
        "expansion": bell_draw(splits[3], (PAIRS, LM), PAIRS ** -0.5, 0.625, (), jnp.float32),
        "box_corners": draw_box_corners(jax.random.fold_in(splits[8], 71), 0),
        "box_offsets": jnp.clip(jax.random.uniform(splits[5], (ATOMS, 3), jnp.float32, -0.5, 0.5) * level_of(splits[5], (ATOMS, 3), ((0, 512),), -0.4, 0.0), -0.5, 0.5),
        "atom_lists": draw_atom_lists(jax.random.fold_in(splits[8], 71), 0),
        "atom_counts": draw_atom_counts(jax.random.fold_in(splits[8], 71), 0),
    }


RELAX = 0.8
INV_RC = 0.5
EXPONENTS = ((0, 0, 0), (1, 0, 0), (0, 1, 0), (0, 0, 1), (1, 1, 0), (0, 1, 1), (1, 0, 1), (2, 0, 0), (0, 2, 0), (0, 0, 2))


def multipole_coefficients(pair_density, expansion):
    moments = jnp.dot(pair_density, expansion, precision=lax.Precision.HIGHEST)
    return jnp.concatenate([moments[:, :7], moments[:, 7:8] - moments[:, 8:9], -moments[:, 7:8] - moments[:, 8:9], 2.0 * moments[:, 8:9]], axis=1)


def axis_factors(anchor, length, corner, centre):
    coord = anchor + jnp.arange(length, dtype=jnp.float32)
    inside = (coord[None, :] >= corner[:, None]) & (coord[None, :] < corner[:, None] + BOX)
    scaled = (coord[None, :] - centre[:, None]) * INV_RC
    bell = jnp.where(inside, jnp.exp(-scaled * scaled), 0.0)
    return (bell, scaled * bell, scaled * scaled * bell)


def compensation_block(anchor, coefficients, centre, corner, valid, shape):
    powers = [axis_factors(anchor[k], shape[k], corner[:, k], centre[:, k]) for k in range(3)]
    weights = coefficients * valid[:, None]
    x_terms = jnp.stack([powers[0][e[0]] for e in EXPONENTS], axis=1) * weights[:, :, None]
    y_terms = jnp.stack([powers[1][e[1]] for e in EXPONENTS], axis=1)
    z_terms = jnp.stack([powers[2][e[2]] for e in EXPONENTS], axis=1)
    count = x_terms.shape[0] * x_terms.shape[1]
    plane = (x_terms[:, :, :, None] * y_terms[:, :, None, :]).reshape(count, shape[0] * shape[1])
    block = lax.dot_general(plane, z_terms.reshape(count, shape[2]), (((0,), (0,)), ((), ())), precision=lax.Precision.HIGHEST)
    return block.reshape(shape)


def refine_axis(padded, axis):
    n = padded.shape[axis] - 2
    lower = lax.slice_in_dim(padded, 0, n, axis=axis)
    middle = lax.slice_in_dim(padded, 1, n + 1, axis=axis)
    upper = lax.slice_in_dim(padded, 2, n + 2, axis=axis)
    even = 0.75 * middle + 0.25 * lower
    odd = 0.75 * middle + 0.25 * upper
    shape = list(middle.shape)
    shape[axis] = 2 * n
    return jnp.stack([even, odd], axis=axis + 1).reshape(shape)


def refine(padded):
    for axis in range(3):
        padded = refine_axis(padded, axis)
    return padded


def restrict(field):
    a, b, c = field.shape[0] // 2, field.shape[1] // 2, field.shape[2] // 2
    return jnp.sum(field.reshape(a, 2, b, 2, c, 2), axis=(1, 3, 5)) * 0.125


def neighbours(padded):
    total = padded[2:, 1:-1, 1:-1] + padded[:-2, 1:-1, 1:-1]
    total = total + padded[1:-1, 2:, 1:-1] + padded[1:-1, :-2, 1:-1]
    return total + padded[1:-1, 1:-1, 2:] + padded[1:-1, 1:-1, :-2]


def apply_operator(padded, scale):
    return scale * (6.0 * padded[1:-1, 1:-1, 1:-1] - neighbours(padded))


def jacobi(field, source, padded, scale):
    return field + (RELAX / (6.0 * scale)) * (source - apply_operator(padded, scale))


def vcycle(level, field, source):
    scale = 0.25 ** level
    if level == LEVELS - 1:
        for sweep in range(COARSE_SWEEPS):
            field = jacobi(field, source, jnp.pad(field, 1), scale)
        return field
    for sweep in range(PRE):
        field = jacobi(field, source, jnp.pad(field, 1), scale)
    rest = source - apply_operator(jnp.pad(field, 1), scale)
    coarse_source = restrict(rest)
    correction = vcycle(level + 1, jnp.zeros_like(coarse_source), coarse_source)
    field = field + refine(jnp.pad(correction, 1))
    for sweep in range(POST):
        field = jacobi(field, source, jnp.pad(field, 1), scale)
    return field


def reference(coarse_density, start_potential, pair_density, expansion, box_corners, box_offsets, atom_lists, atom_counts):
    coefficients = multipole_coefficients(pair_density, expansion)
    corner_all = box_corners.astype(jnp.float32)
    centre_all = corner_all + (BOX - 1) * 0.5 + box_offsets

    def one_domain(domain):
        first = domain // (N_GY * N_GZ)
        second = (domain // N_GZ) % N_GY
        third = domain % N_GZ
        atom_ids = atom_lists[domain]
        valid = (jnp.arange(M_SLOTS, dtype=jnp.int32) < atom_counts[domain]).astype(jnp.float32)
        anchor = ((first * FX).astype(jnp.float32), (second * FY).astype(jnp.float32), (third * FZ).astype(jnp.float32))
        return compensation_block(anchor, coefficients[atom_ids], centre_all[atom_ids], corner_all[atom_ids], valid, (FX, FY, FZ))

    blocks = lax.map(one_domain, jnp.arange(DOMAINS, dtype=jnp.int32))
    compensation = blocks.reshape(N_GX, N_GY, N_GZ, FX, FY, FZ).transpose(0, 3, 1, 4, 2, 5).reshape(NX, NY, NZ)
    total_density = refine(jnp.pad(coarse_density, 1)) + compensation
    potential = start_potential
    for cycle in range(CYCLES):
        potential = vcycle(0, potential, total_density)
    return total_density, potential
```

```python
import itertools

import jax
import jax.numpy as jnp
from jax import lax
from jax.experimental import pallas as pl
from jax.experimental.pallas import tpu as pltpu
from jax.sharding import PartitionSpec as P

F32 = jnp.float32
BF16 = jnp.bfloat16
MESH = pl.DeviceIdType.MESH
ALPHA = 0.8 / 6.0
AXES = ("gx", "gy", "gz")
DIRS = [d for d in itertools.product((-1, 0, 1), repeat=3) if d != (0, 0, 0)]
DIRS.sort(key=lambda d: sum(map(abs, d)))
UP7 = [d for d in itertools.product((0, 1), repeat=3) if d != (0, 0, 0)]
RING = list(range(1, 8))
PHASE2 = [(k, dz) for k in range(8) for dz in (-1, 0, 1) if (k, dz) != (0, 0)]
N_ATOM, N_DIR, N_RING, N_P2 = len(UP7), len(DIRS), len(RING), len(PHASE2)
SEM_V = N_ATOM
SEM_RHO = SEM_V + N_DIR
SEM_F = SEM_RHO + N_DIR
SEM_CYCLE = SEM_F + N_DIR
PER_CYCLE = 2 * N_DIR + N_RING + N_P2
N_SEMS = SEM_CYCLE + 2 * PER_CYCLE


def iota(shape, dim):
    return lax.broadcasted_iota(jnp.int32, shape, dim)


def wrapped(lane, cut, lanes):
    return jnp.where(lane < cut, lane, lane - lanes)


def split(a):
    hi = a.astype(BF16)
    return hi, (a - hi.astype(F32)).astype(BF16)


def dot(a, b):
    return jnp.dot(a, b, preferred_element_type=F32)


def mm(a, m):
    hi, lo = split(a)
    return dot(hi, m) + dot(lo, m)


def restrict_matrix(rows, rcut, cols, ccut):
    fine = wrapped(iota((rows, cols), 0), rcut, rows)
    coarse = wrapped(iota((rows, cols), 1), ccut, cols)
    return jnp.where((fine >> 1) == coarse, 1.0, 0.0).astype(BF16)


def prolong_matrix(rows, rcut, cols, ccut):
    coarse = wrapped(iota((rows, cols), 0), rcut, rows)
    fine = wrapped(iota((rows, cols), 1), ccut, cols)
    centre = fine >> 1
    other = jnp.where((fine & 1) == 0, centre - 1, centre + 1)
    return jnp.where(coarse == centre, 0.75, jnp.where(coarse == other, 0.25, 0.0)).astype(BF16)


def grid_mask(shape, starts, sizes, cut, window):
    x = iota(shape, 0) + starts[0]
    y = iota(shape, 1) + starts[1]
    z = wrapped(iota(shape, 2), cut, shape[2])
    near = (z >= window[0]) & (z < window[1])
    z = z + starts[2]
    inside = (x >= 0) & (x < sizes[0]) & (y >= 0) & (y < sizes[1]) & (z >= 0) & (z < sizes[2])
    return jnp.where(inside & near, 1.0, 0.0)


def neighbours(ref, first, count):
    c = ref[pl.ds(first, count)]
    rows, lanes = c.shape[1], c.shape[2]
    total = ref[pl.ds(first - 1, count)] + ref[pl.ds(first + 1, count)]
    total = total + pltpu.roll(c, 1, 1) + pltpu.roll(c, rows - 1, 1)
    return c, total + pltpu.roll(c, 1, 2) + pltpu.roll(c, lanes - 1, 2)


def expand_rows(es, ye, yo, r0, nr):
    def rows(start):
        return es[:, pl.ds(start, nr), :]

    mid = 0.75 * rows(r0)
    ye[...] = mid + 0.25 * rows(r0 - 1)
    yo[...] = mid + 0.25 * rows(r0 + 1)


def store_pairs(out, index, even, odd):
    n = even.shape[0]
    for h in range(even.shape[1] // 128):
        s = slice(128 * h, 128 * h + 128)
        half = out.at[h] if even.shape[1] > 128 else out
        half[index, pl.ds(0, n, 2), :] = even[:, s]
        half[index, pl.ds(1, n, 2), :] = odd[:, s]


def expand_planes(ye, yo, out, f0, c0, k):
    e, o = 0.75 * ye[k + c0], 0.75 * yo[k + c0]
    store_pairs(out, f0 + 2 * k, e + 0.25 * ye[k + c0 - 1], o + 0.25 * yo[k + c0 - 1])
    store_pairs(out, f0 + 2 * k + 1, e + 0.25 * ye[k + c0 + 1], o + 0.25 * yo[k + c0 + 1])


def halve_rows(ref, start, count):
    return ref[pl.ds(start, count, 2), :] + ref[pl.ds(start + 1, count, 2), :]


def kernel(
    rho, v0, pair, expn, corner, offset, dens, pot,
    vf, v1, ff, wf, zl0, zh0, zs0,
    f1, zl1, zh1, zs1, g1, a0, s0, es0, ye0, yo0, e1, w1, es1, ye1, yo1,
    t2, f2, e2, w2, s1, es2, ye2, yo2,
    x1, xs, y1, f3, e3, w3, s2, ts, es3, ye3, yo3,
    f4, v4, a3, s3,
    at, pln, k0, k1, k2, k3, k4, ss, rs,
):
    gx, gy, gz = (lax.axis_index(a) for a in AXES)
    here = (gx, gy, gz)

    def peer(d):
        return tuple(i if s == 0 else lax.rem(i + (s + 8), 8) for i, s in zip(here, d))

    barrier = pltpu.get_barrier_semaphore()
    reached = []
    for d in DIRS + [(k, 0, 0) for k in RING] + [(0, k, dz) for k, dz in PHASE2]:
        d = tuple(s % 8 for s in d)
        if d not in reached:
            reached.append(d)
    for d in reached:
        pl.semaphore_signal(barrier, inc=1, device_id=peer(d), device_id_type=MESH)

    for ref in (v1.at[0], v1.at[27], g1, f3, e3, f4, v4):
        ref[...] = jnp.zeros(ref.shape, F32)
    k0[...] = grid_mask((28, 48, 256), (16 * gx - 6, 32 * gy - 8, 128 * gz), (128, 256, 1024), 192, (-8, 136))
    k1[...] = grid_mask((16, 32, 128), (8 * gx - 4, 16 * gy - 8, 64 * gz), (64, 128, 512), 96, (-8, 72))
    k2[...] = grid_mask((12, 24, 128), (4 * gx - 4, 8 * gy - 8, 32 * gz), (32, 64, 256), 80, (-24, 56))
    k3[...] = grid_mask((16, 48, 128), (0, -8, 16 * gz), (16, 32, 128), 64, (-24, 40))
    k4[...] = grid_mask((8, 32, 128), (0, -8, 8 * gz), (8, 16, 64), 64, (-16, 24))

    vf[6:22, 8:40, 0:128] = v0[...]
    f1[0, 4:12, 8:24, 0:64] = rho[...]

    hi_prec = lax.Precision.HIGHEST
    m = iota((9, 128), 0)
    c = iota((9, 128), 1)
    one = jnp.where((c < 7) & (m == c), 1.0, 0.0)
    one = one + jnp.where((c == 7) & (m == 7), 1.0, 0.0) - jnp.where((c == 7) & (m == 8), 1.0, 0.0)
    one = one - jnp.where((c == 8) & (m >= 7), 1.0, 0.0) + jnp.where((c == 9) & (m == 8), 2.0, 0.0)
    moments = jnp.dot(pair[...], expn[...], precision=hi_prec)
    packed = jnp.dot(moments, one, precision=hi_prec)
    corners = corner[...].astype(F32)
    centres = corners + 5.5 + offset[...]
    p3 = iota((3, 128), 0)
    l3 = iota((3, 128), 1)
    packed = packed + jnp.dot(centres, jnp.where(l3 == p3 + 10, 1.0, 0.0), precision=hi_prec)
    packed = packed + jnp.dot(corners, jnp.where(l3 == p3 + 13, 1.0, 0.0), precision=hi_prec)
    at[0:16, :] = packed

    pl.semaphore_wait(barrier, len(reached))

    def rcopy(src, dst, k, d):
        return pltpu.make_async_remote_copy(
            src_ref=src, dst_ref=dst, send_sem=ss.at[k], recv_sem=rs.at[k], device_id=peer(d), device_id_type=MESH
        )

    def atom_copies():
        return [
            rcopy(at.at[0:16], at.at[16 * k + 16 : 16 * k + 32], k, d) for k, d in enumerate(UP7)
        ]

    def frame_slices(d, nx, hx, ny):
        src, dst = [], []
        for s, n, h, o in ((d[0], nx, hx, hx), (d[1], ny, 8, 8)):
            if s == 0:
                src.append(slice(o, o + n))
                dst.append(slice(o, o + n))
            elif s > 0:
                src.append(slice(o + n - h, o + n))
                dst.append(slice(0, h))
            else:
                src.append(slice(o, o + h))
                dst.append(slice(o + n, o + n + h))
        return tuple(src), tuple(dst)

    def copies0(frame, q, base):
        out = []
        for k, d in enumerate(DIRS):
            src, dst = frame_slices(d, 16, 6, 32)
            if d[2] == 0:
                out.append(rcopy(frame.at[src + (slice(0, 128),)], frame.at[dst + (slice(0, 128),)], base + k, d))
            else:
                rows = slice(src[1].start - 8, src[1].stop - 8)
                zr = zh0 if d[2] > 0 else zl0
                out.append(rcopy(zs0.at[q, 1 if d[2] > 0 else 0, rows], zr.at[q, 1 - d[0], dst[1]], base + k, d))
        return out

    def copies1(q, base):
        out = []
        for k, d in enumerate(DIRS):
            src, dst = frame_slices(d, 8, 4, 16)
            if d[2] == 0:
                out.append(rcopy(f1.at[(q,) + src], f1.at[(q,) + dst], base + k, d))
            else:
                rows = slice(src[1].start - 8, src[1].stop - 8)
                zr = zh1 if d[2] > 0 else zl1
                out.append(rcopy(zs1.at[q, rows], zr.at[q, 1 - d[0], dst[1]], base + k, d))
        return out

    def copies2(q, base):
        mine = t2.at[q, 1, 1, 8:16]
        return [
            rcopy(mine, t2.at[q, 1 - d[2], 1 - d[0], 8 * (1 - d[1]) : 8 * (1 - d[1]) + 8], base + k, d)
            for k, d in enumerate(DIRS)
        ]

    def copies3a(q, base):
        return [rcopy(x1.at[q, 0], x1.at[q, n], base + k, (n, 0, 0)) for k, n in enumerate(RING)]

    def copies3b(q, base):
        return [
            rcopy(y1.at[q, 1, gy], y1.at[q, 1 - dz, gy], base + k, (0, n, dz)) for k, (n, dz) in enumerate(PHASE2)
        ]

    def start(copies):
        for item in copies:
            item.start()

    def wait_recv(copies):
        for item in copies:
            item.wait_recv()

    def wait_send(copies):
        for item in copies:
            item.wait_send()

    def pack0(frame, q):
        lane = iota((32, 128), 1)
        lo = hi = jnp.zeros((32, 128), F32)
        for x in range(16):
            t = frame[6 + x, 8:40, 0:128]
            if x:
                t = pltpu.roll(t, 8 * x, 1)
            h = (8 * x - 8) % 128
            lo = jnp.where((lane >= 8 * x) & (lane < 8 * x + 8), t, lo)
            hi = jnp.where((lane >= h) & (lane < h + 8), t, hi)
        zs0[q, 0] = lo
        zs0[q, 1] = hi

    def unpack0(frame, q):
        lane = iota((48, 128), 1)

        def body(i, carry):
            slot = jnp.where(i < 6, 0, jnp.where(i < 22, 1, 2))
            sx = jnp.where(i < 6, i + 10, jnp.where(i < 22, i - 6, i - 22))
            t = jnp.where((lane >= 8 * sx) & (lane < 8 * sx + 8), zl0[q, slot], zh0[q, slot])
            t = pltpu.roll(t, lax.rem(128 - 8 * sx, 128), 1)
            frame[i, :, 0:128] = frame[i, :, 0:128] * k0[i, :, 0:128]
            frame[i, :, 128:256] = jnp.where((lane < 8) | (lane >= 120), t, 0.0) * k0[i, :, 128:256]
            return carry

        lax.fori_loop(0, 28, body, 0)

    def pack1(q):
        lane = iota((16, 128), 1)
        out = jnp.zeros((16, 128), F32)
        for x in range(8):
            t = f1[q, 4 + x, 8:24, :]
            lo = t if x == 0 else pltpu.roll(t, 16 * x, 1)
            hi = t if x == 3 else pltpu.roll(t, (16 * x - 48) % 128, 1)
            out = jnp.where((lane >= 16 * x) & (lane < 16 * x + 8), lo, out)
            out = jnp.where((lane >= 16 * x + 8) & (lane < 16 * x + 16), hi, out)
        zs1[q] = out

    def unpack1(q):
        lane = iota((32, 128), 1)
        for i in range(16):
            slot = 0 if i < 4 else 1 if i < 12 else 2
            sx = (4 + i) % 8 if i < 4 else (i - 4) % 8
            lo = zl1[q, slot]
            hi = zh1[q, slot]
            if (64 - 16 * sx) % 128:
                lo = pltpu.roll(lo, (64 - 16 * sx) % 128, 1)
            if (112 - 16 * sx) % 128:
                hi = pltpu.roll(hi, (112 - 16 * sx) % 128, 1)
            t = jnp.where(lane < 64, f1[q, i], jnp.where(lane < 72, lo, jnp.where(lane >= 120, hi, 0.0)))
            f1[q, i] = t * k1[i]

    def unpack2(q):
        lane = iota((24, 128), 1)
        for i in range(12):
            slot, sx = i // 4, i % 4
            below, mid, above = t2[q, 0, slot], t2[q, 1, slot], t2[q, 2, slot]
            if sx:
                mid = pltpu.roll(mid, 128 - 32 * sx, 1)
            if sx != 1:
                above = pltpu.roll(above, (32 - 32 * sx) % 128, 1)
            if sx != 3:
                below = pltpu.roll(below, 96 - 32 * sx, 1)
            t = jnp.where(lane < 32, mid, jnp.where(lane < 64, above, jnp.where(lane >= 96, below, 0.0)))
            f2[i] = t * k2[i]

    def unpack3(q):
        lane = iota((64, 128), 1)
        keep = k3[0, 8:9, :]

        def body(g, carry):
            def turned(slot, target):
                return pltpu.roll(y1[q, slot].reshape(64, 128), lax.rem(128 + target - 16 * g, 128), 1)

            t = jnp.where(lane < 16, turned(1, 0), 0.0)
            t = jnp.where((lane >= 16) & (lane < 32), turned(2, 16), t)
            t = jnp.where(lane >= 112, turned(0, 112), t) * keep
            for h in range(8):
                for xl in range(2):
                    f3[4 + 2 * g + xl, 8 + 4 * h : 12 + 4 * h, :] = t[8 * h + 4 * xl : 8 * h + 4 * xl + 4]
            return carry

        lax.fori_loop(0, 8, body, 0)

    def prolong0(source):
        es0[...] = mm(source.reshape(512, 128), prolong_matrix(128, 96, 256, 192)).reshape(16, 32, 256)

        def rows(i, carry):
            mid = 0.75 * es0[i, 4:28, :]
            ye0[i] = mid + 0.25 * es0[i, 3:27, :]
            yo0[i] = mid + 0.25 * es0[i, 5:29, :]
            return carry

        lax.fori_loop(0, 16, rows, 0)

        def planes(k, carry):
            expand_planes(ye0, yo0, wf, 0, 1, k)
            return carry

        lax.fori_loop(0, 14, planes, 0)

    atoms = atom_copies()
    start(atoms)
    pack1(0)
    rho_copies = copies1(0, SEM_RHO)
    start(rho_copies)
    pack0(vf, 0)
    v_copies = copies0(vf, 0, SEM_V)
    start(v_copies)

    wait_recv(rho_copies)
    wait_send(rho_copies)
    unpack1(0)
    prolong0(f1[0])

    wait_recv(atoms)
    by_atom = at[...]
    by_param = by_atom.T

    def factor(coord, centre, low):
        u = (coord - centre) * 0.5
        e = jnp.where((coord >= low) & (coord < low + 12.0), jnp.exp(-u * u), 0.0)
        return u, e

    def row(k):
        return by_param[k : k + 1, :]

    def coordinates(shape, dim, first):
        return (iota(shape, dim) + first).astype(F32)

    ux, ex = factor(coordinates((16, 128), 0, 16 * gx), row(10), row(13))
    uy, ey = factor(coordinates((32, 128), 0, 32 * gy), row(11), row(14))
    uz, ez = factor(coordinates((128, 128), 1, 128 * gz), by_atom[:, 12:13], by_atom[:, 15:16])
    uex = ux * ex
    p00 = row(0) * ex + row(1) * uex + row(7) * (ux * uex)
    p01 = row(2) * ex + row(4) * uex
    p02 = row(8) * ex
    p10 = row(3) * ex + row(6) * uex
    p11 = row(5) * ex
    p20 = row(9) * ex
    uey = uy * ey
    uuey = uy * uey
    for x in range(16):
        s = slice(x, x + 1)
        pln[32 * x : 32 * x + 32, 0:128] = p00[s] * ey + p01[s] * uey + p02[s] * uuey
        pln[32 * x : 32 * x + 32, 128:256] = p10[s] * ey + p11[s] * uey
        pln[32 * x : 32 * x + 32, 256:384] = p20[s] * ey
    uez = uz * ez
    z_hi, z_lo = split(jnp.concatenate([ez, uez, uz * uez], axis=0))
    p_hi, p_lo = split(pln[...])
    block = dot(p_hi, z_hi) + dot(p_hi, z_lo) + dot(p_lo, z_hi)
    block = block.reshape(16, 32, 128) + wf[0, 6:22, 8:40, :]
    dens[...] = block
    ff[6:22, 8:40, 0:128] = block

    pack0(ff, 1)
    f_copies = copies0(ff, 1, SEM_F)
    start(f_copies)
    wait_recv(v_copies)
    wait_send(v_copies)
    unpack0(vf, 0)
    wait_recv(f_copies)
    wait_send(f_copies)
    unpack0(ff, 1)

    def cycle(q, carry):
        base = SEM_CYCLE + q * PER_CYCLE
        c1 = copies1(q + 1, base)
        c2 = copies2(q, base + N_DIR)
        c3a = copies3a(q, base + 2 * N_DIR)
        c3b = copies3b(q, base + 2 * N_DIR + N_RING)

        def pre(i, carry):
            c, nb = neighbours(vf, 2 * i + 1, 2)
            s = pl.ds(2 * i + 1, 2)
            v1[s] = (0.2 * c + ALPHA * (ff[s] + nb)) * k0[s]
            return carry

        lax.fori_loop(0, 13, pre, 0)

        def residual(k, carry):
            c, nb = neighbours(v1, 4 + 2 * k, 2)
            r = ff[pl.ds(4 + 2 * k, 2)] - 6.0 * c + nb
            r = r[0] + r[1]
            s0[0] = r[:, 0:128]
            s0[1] = r[:, 128:256]
            a0[k] = jnp.concatenate([halve_rows(s0.at[h], 0, 24) for h in range(2)], axis=1)
            return carry

        lax.fori_loop(0, 10, residual, 0)
        g = 0.125 * mm(a0[...].reshape(240, 256), restrict_matrix(256, 192, 128, 96))
        g1[:, 4:28, :] = g.reshape(10, 24, 128)
        g1[...] = g1[...] * k1[3:13]
        f1[q + 1, 4:12, 8:24, :] = g1[1:9, 8:24, :]

        c, nb = neighbours(g1, 1, 8)
        r = (0.2 * c + ALPHA * nb).reshape(4, 2, 32, 128)
        s1[...] = r[:, 0] + r[:, 1]
        parts = jnp.concatenate(
            [s1[x, pl.ds(8, 8, 2), :] + s1[x, pl.ds(9, 8, 2), :] for x in range(4)], axis=1
        )
        row_at = iota((512, 128), 0)
        col_at = iota((512, 128), 1)
        lane_at = row_at & 127
        m2 = jnp.where((lane_at < 64) & ((row_at >> 7) * 32 + (lane_at >> 1) == col_at), 1.0, 0.0).astype(BF16)
        t2[q, 1, 1, 8:16] = 0.125 * mm(parts, m2)
        start(c2)
        pack1(q + 1)
        start(c1)

        wait_recv(c2)
        unpack2(q)
        c, nb = neighbours(f2, 4, 4)
        r = (0.2 * c + ALPHA * nb).reshape(2, 2, 24, 128)
        r = r[:, 0] + r[:, 1]
        s2[0:8] = r[0, 8:16]
        s2[8:16] = r[1, 8:16]
        row_at = iota((128, 128), 0)
        col_at = iota((128, 128), 1)
        m3 = jnp.where((row_at < 32) & (16 * gx + (row_at >> 1) == col_at), 1.0, 0.0).astype(BF16)
        x1[q, 0] = 0.125 * mm(halve_rows(s2, 0, 8), m3)
        start(c3a)
        wait_recv(c3a)
        total = x1[q, 0]
        for n in RING:
            total = total + x1[q, n]
        y1[q, 1, gy] = total
        start(c3b)
        wait_recv(c3b)
        unpack3(q)

        c, nb = neighbours(f3, 4, 16)
        r = (0.2 * c + ALPHA * nb).reshape(8, 2, 48, 128)
        s3[...] = r[:, 0] + r[:, 1]
        a3[...] = s3[:, pl.ds(8, 16, 2), :] + s3[:, pl.ds(9, 16, 2), :]
        g = 0.125 * mm(a3[...].reshape(128, 128), restrict_matrix(128, 64, 128, 64))
        f4[1:9, 8:24, :] = g.reshape(8, 16, 128) * k4[:, 8:24, :]

        weight4, weight3, weight2, weight1 = (ALPHA * 4.0**level for level in (4, 3, 2, 1))
        v4[1:9] = weight4 * f4[1:9]
        for _ in range(3):
            c, nb = neighbours(v4, 1, 8)
            v4[1:9] = (0.2 * c + ALPHA * nb + weight4 * f4[1:9]) * k4[...]

        es3[...] = mm(v4[...].reshape(320, 128), prolong_matrix(128, 64, 128, 64)).reshape(10, 32, 128)
        expand_rows(es3, ye3, yo3, 4, 24)
        for k in range(8):
            expand_planes(ye3, yo3, w3, 4, 1, k)
        rhs = weight3 * f3[4:20]
        e3[4:20] = (rhs + w3[4:20]) * k3[...]
        c, nb = neighbours(e3, 4, 16)
        e3[4:20] = (0.2 * c + ALPHA * nb + rhs) * k3[...]

        near = e3[pl.ds(2 * gx + 1, 8)].reshape(384, 128)
        es2[...] = mm(near, prolong_matrix(128, 64, 128, 80)).reshape(8, 48, 128)
        expand_rows(es2, ye2, yo2, 4 * gy + 4, 12)
        for k in range(6):
            expand_planes(ye2, yo2, w2, 0, 1, k)
        rhs = weight2 * f2[...]
        e2[...] = (rhs + w2[...]) * k2[...]
        c, nb = neighbours(e2, 1, 10)
        e2[1:11] = (0.2 * c + ALPHA * nb + rhs[1:11]) * k2[1:11]

        es1[...] = mm(e2[...].reshape(288, 128), prolong_matrix(128, 80, 128, 96)).reshape(12, 24, 128)
        expand_rows(es1, ye1, yo1, 4, 16)
        for k in range(8):
            expand_planes(ye1, yo1, w1, 0, 2, k)
        wait_recv(c1)
        wait_send(c1)
        unpack1(q + 1)
        rhs = weight1 * f1[q + 1]
        e1[...] = (rhs + w1[...]) * k1[...]
        c, nb = neighbours(e1, 1, 14)
        e1[1:15] = (0.2 * c + ALPHA * nb + rhs[1:15]) * k1[1:15]

        prolong0(e1[...])

        def correct(i, carry):
            s = pl.ds(2 * i, 2)
            for h in range(2):
                z = slice(128 * h, 128 * h + 128)
                v1[s, :, z] = (v1[s, :, z] + wf[h, s]) * k0[s, :, z]
            return carry

        lax.fori_loop(0, 14, correct, 0)

        def post(i, carry):
            c, nb = neighbours(v1, 2 * i + 1, 2)
            s = pl.ds(2 * i + 1, 2)
            vf[s] = (0.2 * c + ALPHA * (ff[s] + nb)) * k0[s]
            return carry

        lax.fori_loop(0, 13, post, 0)
        wait_send(c2)
        wait_send(c3a)
        wait_send(c3b)
        return carry

    lax.fori_loop(0, 2, cycle, 0)
    pot[...] = vf[6:22, 8:40, 0:128]
    wait_send(atoms)


def scratch():
    def vm(*shape):
        return pltpu.VMEM(shape, F32)

    return [
        vm(28, 48, 256), vm(28, 48, 256), vm(28, 48, 256), vm(2, 28, 48, 128),
        vm(2, 3, 48, 128), vm(2, 3, 48, 128), vm(2, 2, 32, 128),
        vm(3, 16, 32, 128), vm(3, 3, 32, 128), vm(3, 3, 32, 128), vm(3, 16, 128),
        vm(10, 32, 128), vm(10, 24, 256), vm(2, 48, 128), vm(16, 32, 256), vm(16, 24, 256), vm(16, 24, 256),
        vm(16, 32, 128), vm(16, 32, 128), vm(12, 24, 128), vm(12, 16, 128), vm(12, 16, 128),
        vm(2, 3, 3, 24, 128), vm(12, 24, 128), vm(12, 24, 128), vm(12, 24, 128), vm(4, 32, 128),
        vm(8, 48, 128), vm(8, 12, 128), vm(8, 12, 128),
        vm(2, 8, 8, 128), vm(2, 8, 128), vm(2, 3, 8, 8, 128), vm(24, 48, 128), vm(24, 48, 128), vm(24, 48, 128),
        vm(16, 128), vm(64, 128), vm(10, 32, 128), vm(10, 24, 128), vm(10, 24, 128),
        vm(10, 32, 128), vm(10, 32, 128), vm(8, 16, 128), vm(8, 48, 128),
        vm(128, 128), vm(512, 384),
        vm(28, 48, 256), vm(16, 32, 128), vm(12, 24, 128), vm(16, 48, 128), vm(8, 32, 128),
        pltpu.SemaphoreType.DMA((N_SEMS,)), pltpu.SemaphoreType.DMA((N_SEMS,)),
    ]


def per_device(coarse_density, start_potential, pair_density, expansion, box_corners, box_offsets, lists, counts):
    del lists, counts
    block = jax.ShapeDtypeStruct((16, 32, 128), F32)
    vmem = pl.BlockSpec(memory_space=pltpu.VMEM)
    return pl.pallas_call(
        kernel,
        out_shape=(block, block),
        in_specs=[vmem] * 6,
        out_specs=(vmem, vmem),
        scratch_shapes=scratch(),
        compiler_params=pltpu.CompilerParams(
            collective_id=0, has_side_effects=True, vmem_limit_bytes=40 * 2**20
        ),
    )(coarse_density, start_potential, pair_density, expansion, box_corners, box_offsets)


def solution(mesh):
    everywhere = P(AXES, None)
    in_specs = (P(*AXES), P(*AXES), everywhere, P(), everywhere, everywhere, everywhere, P(AXES))
    return jax.shard_map(
        per_device, mesh=mesh, in_specs=in_specs, out_specs=(P(*AXES), P(*AXES)), check_vma=False
    )
```

```python
import itertools

import jax
import jax.numpy as jnp
from jax import lax
from jax.experimental import pallas as pl
from jax.experimental.pallas import tpu as pltpu
from jax.sharding import PartitionSpec as P

F32 = jnp.float32
BF16 = jnp.bfloat16
MESH = pl.DeviceIdType.MESH
ALPHA = 0.8 / 6.0
AXES = ("gx", "gy", "gz")
DIRS = [d for d in itertools.product((-1, 0, 1), repeat=3) if d != (0, 0, 0)]
DIRS.sort(key=lambda d: -sum(map(abs, d)))
XY_DIRS = [d for d in DIRS if d[2] == 0 and d[0] != 0]
UP7 = [d for d in itertools.product((0, 1), repeat=3) if d != (0, 0, 0)]
RING = [4, 3, 5, 2, 6, 1, 7]
X_NEAR = [1, -1, 2, -2]
YZ_NEAR = [d for d in DIRS if d[0] == 0]
N_ATOM, N_DIR, N_RING = len(UP7), len(DIRS), len(RING)
SEM_V = N_ATOM
SEM_RHO = SEM_V + N_DIR
SEM_F = SEM_RHO + N_DIR
SEM_LATE = SEM_F + N_DIR
SEM_CYCLE = SEM_LATE + len(XY_DIRS)
PER_CYCLE = 2 * N_DIR + 2 * N_RING + len(X_NEAR) + len(YZ_NEAR)
N_SEMS = SEM_CYCLE + 2 * PER_CYCLE


def iota(shape, dim):
    return lax.broadcasted_iota(jnp.int32, shape, dim)


def wrapped(lane, cut, lanes):
    return jnp.where(lane < cut, lane, lane - lanes)


def split(a):
    hi = a.astype(BF16)
    return hi, (a - hi.astype(F32)).astype(BF16)


def dot(a, b):
    return jnp.dot(a, b, preferred_element_type=F32)


def mm(a, m):
    hi, lo = split(a)
    return dot(hi, m) + dot(lo, m)


def restrict_matrix(rows, rcut, cols, ccut):
    fine = wrapped(iota((rows, cols), 0), rcut, rows)
    coarse = wrapped(iota((rows, cols), 1), ccut, cols)
    return jnp.where((fine >> 1) == coarse, 1.0, 0.0).astype(BF16)


def prolong_matrix(rows, rcut, cols, ccut):
    coarse = wrapped(iota((rows, cols), 0), rcut, rows)
    fine = wrapped(iota((rows, cols), 1), ccut, cols)
    centre = fine >> 1
    other = jnp.where((fine & 1) == 0, centre - 1, centre + 1)
    return jnp.where(coarse == centre, 0.75, jnp.where(coarse == other, 0.25, 0.0)).astype(BF16)


def grid_mask(shape, starts, sizes, cut, window):
    x = iota(shape, 0) + starts[0]
    y = iota(shape, 1) + starts[1]
    z = wrapped(iota(shape, 2), cut, shape[2])
    near = (z >= window[0]) & (z < window[1])
    z = z + starts[2]
    inside = (x >= 0) & (x < sizes[0]) & (y >= 0) & (y < sizes[1]) & (z >= 0) & (z < sizes[2])
    return jnp.where(inside & near, 1.0, 0.0)


def neighbours(ref, first, count):
    c = ref[pl.ds(first, count)]
    rows, lanes = c.shape[1], c.shape[2]
    total = ref[pl.ds(first - 1, count)] + ref[pl.ds(first + 1, count)]
    total = total + pltpu.roll(c, 1, 1) + pltpu.roll(c, rows - 1, 1)
    return c, total + pltpu.roll(c, 1, 2) + pltpu.roll(c, lanes - 1, 2)


def expand_rows(es, ye, yo, r0, nr):
    def rows(start):
        return es[:, pl.ds(start, nr), :]

    mid = 0.75 * rows(r0)
    ye[...] = mid + 0.25 * rows(r0 - 1)
    yo[...] = mid + 0.25 * rows(r0 + 1)


def plane_pair(ye, yo, c0, k):
    pairs = []
    e, o = 0.75 * ye[k + c0], 0.75 * yo[k + c0]
    for side in (k + c0 - 1, k + c0 + 1):
        pairs.append((e + 0.25 * ye[side], o + 0.25 * yo[side]))
    return pairs


def expand_planes(ye, yo, out, f0, c0, k):
    for x, (even, odd) in enumerate(plane_pair(ye, yo, c0, k)):
        n = even.shape[0]
        out[f0 + 2 * k + x, pl.ds(0, n, 2), :] = even
        out[f0 + 2 * k + x, pl.ds(1, n, 2), :] = odd


def both(ref, i):
    return jnp.concatenate([ref[0, i], ref[1, i]], axis=1)


def spread(c, before, after):
    rows, lanes = c.shape
    total = before + after + pltpu.roll(c, 1, 0) + pltpu.roll(c, rows - 1, 0)
    return total + pltpu.roll(c, 1, 1) + pltpu.roll(c, lanes - 1, 1)


def halve_rows(ref, start, count):
    return ref[pl.ds(start, count, 2), :] + ref[pl.ds(start + 1, count, 2), :]


def kernel(
    rho_hbm, v0_hbm, pair, expn_t, corner_t, offset_t, dens, pot,
    vf, v1, ff, zl0, zh0, zs0, rho,
    f1, zl1, zh1, zs1, g1, a0, s0, es0, ye0, yo0, e1, w1, es1, ye1, yo1,
    t2, f2, e2, w2, s1, es2, ye2, yo2,
    x1, y1, f3, e3, w3, s2, a2, g3, s4, es3, ye3, yo3,
    xa, yb, ts, f4, v4,
    at, tp, pln, k0, ke, ko, k1, k2, k3, kg, k4, local, ss, rs,
):
    gx, gy, gz = (lax.axis_index(a) for a in AXES)
    here = (gx, gy, gz)

    def peer(d):
        return tuple(i if s == 0 else lax.rem(i + (s + 8), 8) for i, s in zip(here, d))

    rho_in = pltpu.make_async_copy(rho_hbm, rho, local.at[0])
    v0_in = pltpu.make_async_copy(v0_hbm, vf.at[6:22, 8:40, 0:128], local.at[1])
    rho_in.start()
    v0_in.start()
    barrier = pltpu.get_barrier_semaphore()
    reached = []
    for d in DIRS[::-1] + [(k, 0, 0) for k in RING] + [(0, k, 0) for k in RING]:
        d = tuple(s % 8 for s in d)
        if d not in reached:
            reached.append(d)
    for d in reached:
        pl.semaphore_signal(barrier, inc=1, device_id=peer(d), device_id_type=MESH)

    def pack0(frame, q):
        lane = iota((32, 128), 1)
        lo = hi = jnp.zeros((32, 128), F32)
        for x in range(16):
            t = frame[6 + x, 8:40, 0:128]
            if x:
                t = pltpu.roll(t, 8 * x, 1)
            h = (8 * x - 8) % 128
            lo = jnp.where((lane >= 8 * x) & (lane < 8 * x + 8), t, lo)
            hi = jnp.where((lane >= h) & (lane < h + 8), t, hi)
        zs0[q, 0] = lo
        zs0[q, 1] = hi

    def pack1(q):
        lane = iota((16, 128), 1)
        out = jnp.zeros((16, 128), F32)
        for x in range(8):
            t = f1[q, 4 + x, 8:24, :]
            lo = t if x == 0 else pltpu.roll(t, 16 * x, 1)
            hi = t if x == 3 else pltpu.roll(t, (16 * x - 48) % 128, 1)
            out = jnp.where((lane >= 16 * x) & (lane < 16 * x + 8), lo, out)
            out = jnp.where((lane >= 16 * x + 8) & (lane < 16 * x + 16), hi, out)
        zs1[q] = out

    hi_prec = lax.Precision.HIGHEST
    m = iota((9, 128), 0)
    c = iota((9, 128), 1)
    one = jnp.where((c < 7) & (m == c), 1.0, 0.0)
    one = one + jnp.where((c == 7) & (m == 7), 1.0, 0.0) - jnp.where((c == 7) & (m == 8), 1.0, 0.0)
    one = one - jnp.where((c == 8) & (m >= 7), 1.0, 0.0) + jnp.where((c == 9) & (m == 8), 2.0, 0.0)
    moments = lax.dot_general(
        pair[...], expn_t[...], (((1,), (1,)), ((), ())), precision=hi_prec, preferred_element_type=F32
    )
    packed = jnp.dot(moments, one, precision=hi_prec)
    corners = corner_t[...].astype(F32)
    tp[...] = jnp.zeros(tp.shape, F32)
    tp[10:13, 0:16] = corners + 5.5 + offset_t[...]
    tp[13:16, 0:16] = corners
    at[0:16, :] = packed + tp[...].T[0:16]
    rho_in.wait()
    f1[0, 4:12, 8:24, 0:64] = rho[...]
    pack1(0)
    v0_in.wait()
    pack0(vf, 0)

    pl.semaphore_wait(barrier, len(reached))

    def rcopy(src, dst, k, d):
        return pltpu.make_async_remote_copy(
            src_ref=src, dst_ref=dst, send_sem=ss.at[k], recv_sem=rs.at[k], device_id=peer(d), device_id_type=MESH
        )

    def atom_copies():
        return [
            rcopy(at.at[0:16], at.at[16 * k + 16 : 16 * k + 32], k, d) for k, d in enumerate(UP7)
        ]

    def frame_slices(d, nx, hx, ny, part):
        near, far = part
        src, dst = [], []
        for s, n, h, o, a, b in ((d[0], nx, hx, hx, near, far), (d[1], ny, 8, 8, 0, 8)):
            if s == 0:
                src.append(slice(o, o + n))
                dst.append(slice(o, o + n))
            elif s > 0:
                src.append(slice(o + n - b, o + n - a))
                dst.append(slice(h - b, h - a))
            else:
                src.append(slice(o + a, o + b))
                dst.append(slice(o + n + a, o + n + b))
        return tuple(src), tuple(dst)

    def copies0(frame, q, base, part):
        out = []
        for k, d in enumerate(DIRS):
            src, dst = frame_slices(d, 16, 6, 32, part)
            if d[2] == 0:
                out.append(rcopy(frame.at[src + (slice(0, 128),)], frame.at[dst + (slice(0, 128),)], base + k, d))
            else:
                rows = slice(src[1].start - 8, src[1].stop - 8)
                zr = zh0 if d[2] > 0 else zl0
                out.append(rcopy(zs0.at[q, 1 if d[2] > 0 else 0, rows], zr.at[q, 1 - d[0], dst[1]], base + k, d))
        return out

    def late_copies():
        out = []
        for k, d in enumerate(XY_DIRS):
            src, dst = frame_slices(d, 16, 6, 32, (3, 5))
            out.append(rcopy(ff.at[src + (slice(0, 128),)], ff.at[dst + (slice(0, 128),)], SEM_LATE + k, d))
        return out

    def copies1(q, base, part):
        out = []
        for k, d in enumerate(DIRS):
            src, dst = frame_slices(d, 8, 4, 16, part)
            if d[2] == 0:
                out.append(rcopy(f1.at[(q,) + src], f1.at[(q,) + dst], base + k, d))
            else:
                rows = slice(src[1].start - 8, src[1].stop - 8)
                zr = zh1 if d[2] > 0 else zl1
                out.append(rcopy(zs1.at[q, rows], zr.at[q, 1 - d[0], dst[1]], base + k, d))
        return out

    def copies2(q, base):
        mine = t2.at[q, 1, 1, 8:16]
        return [
            rcopy(mine, t2.at[q, 1 - d[2], 1 - d[0], 8 * (1 - d[1]) : 8 * (1 - d[1]) + 8], base + k, d)
            for k, d in enumerate(DIRS)
        ]

    def copies3a(q, base):
        return [rcopy(x1.at[q, 0], x1.at[q, k + 1], base + k, (n, 0, 0)) for k, n in enumerate(X_NEAR)]

    def copies3b(q, base):
        return [
            rcopy(y1.at[q, 1, 8:16], y1.at[q, 1 - d[2], 8 * (1 - d[1]) : 8 * (1 - d[1]) + 8], base + k, d)
            for k, d in enumerate(YZ_NEAR)
        ]

    def copies4a(q, base):
        return [rcopy(xa.at[q, gx], xa.at[q, gx], base + k, (n, 0, 0)) for k, n in enumerate(RING)]

    def copies4b(q, base):
        return [rcopy(yb.at[q, gy], yb.at[q, gy], base + k, (0, n, 0)) for k, n in enumerate(RING)]

    def start(copies):
        for item in copies:
            item.start()

    def wait_recv(copies):
        for item in copies:
            item.wait_recv()

    def wait_send(copies):
        for item in copies:
            item.wait_send()

    def in_x(i):
        x = 16 * gx + i - 6
        return jnp.where((x >= 0) & (x < 128), 1.0, 0.0)

    def unpack0(frame, q, halo, own):
        lane = iota((48, 128), 1)
        keep = (lane < 8) | (lane >= 120)

        def beside(slot, sx, i):
            t = jnp.where((lane >= 8 * sx) & (lane < 8 * sx + 8), zl0[q, slot], zh0[q, slot])
            t = pltpu.roll(t, lax.rem(128 - 8 * sx, 128), 1)
            return jnp.where(keep, t, 0.0) * (k0[:, 128:256] * in_x(i))

        for i in halo:
            below = i < 6
            frame[i, :, 0:128] = frame[i, :, 0:128] * (k0[:, 0:128] * in_x(i))
            frame[i, :, 128:256] = beside(0 if below else 2, jnp.int32(i + 10 if below else i - 22), i)

        def body(k, carry):
            values = [(i, beside(1, i - 6, i)) for i in (2 * k + 6, 2 * k + 7)]
            for i, value in values:
                frame[i, :, 128:256] = value
                for rows in (slice(0, 8), slice(40, 48)):
                    frame[i, rows, 0:128] = frame[i, rows, 0:128] * k0[rows, 0:128]
            return carry

        if own:
            lax.fori_loop(0, 8, body, 0)

    def unpack1(q):
        lane = iota((32, 128), 1)
        for i in range(16) if not isinstance(q, int) else range(3, 13):
            slot = 0 if i < 4 else 1 if i < 12 else 2
            sx = (4 + i) % 8 if i < 4 else (i - 4) % 8
            lo = zl1[q, slot]
            hi = zh1[q, slot]
            if (64 - 16 * sx) % 128:
                lo = pltpu.roll(lo, (64 - 16 * sx) % 128, 1)
            if (112 - 16 * sx) % 128:
                hi = pltpu.roll(hi, (112 - 16 * sx) % 128, 1)
            t = jnp.where(lane < 64, f1[q, i], jnp.where(lane < 72, lo, jnp.where(lane >= 120, hi, 0.0)))
            f1[q, i] = t * k1[i]

    def unpack2(q):
        lane = iota((24, 128), 1)
        for i in range(12):
            slot, sx = i // 4, i % 4
            below, mid, above = t2[q, 0, slot], t2[q, 1, slot], t2[q, 2, slot]
            if sx:
                mid = pltpu.roll(mid, 128 - 32 * sx, 1)
            if sx != 1:
                above = pltpu.roll(above, (32 - 32 * sx) % 128, 1)
            if sx != 3:
                below = pltpu.roll(below, 96 - 32 * sx, 1)
            t = jnp.where(lane < 32, mid, jnp.where(lane < 64, above, jnp.where(lane >= 96, below, 0.0)))
            f2[i] = t * k2[i]

    def unpack3(q):
        lane = iota((24, 128), 1)
        for dx in range(-2, 3):
            shift = 16 * lax.rem(gx + (dx + 8), 8)

            def turned(slot, target):
                return pltpu.roll(y1[q, slot], lax.rem(128 + target - shift, 128), 1)

            t = jnp.where(lane < 16, turned(1, 0), 0.0)
            t = jnp.where((lane >= 16) & (lane < 32), turned(2, 16), t)
            t = jnp.where(lane >= 112, turned(0, 112), t)
            for y in range(3):
                for x in range(2):
                    f3[2 * dx + 4 + x, 4 + 4 * y : 8 + 4 * y, :] = t[8 * y + 4 * x : 8 * y + 4 * x + 4]
        f3[...] = f3[...] * k3[...]

    def unpack4(q):
        lane = iota((64, 128), 1)
        for y in range(2):
            t = pltpu.roll(yb[q].reshape(64, 128), 120 - 32 * y, 1)
            ts[y] = jnp.where((lane < 16) | (lane >= 120), t, 0.0)
        for x in range(8):
            for y in range(2):
                f4[x, pl.ds(8 + y, 8, 2), :] = ts[y, pl.ds(x, 8, 8), :]

    def prolong0(source, first, add):
        es0[...] = mm(source.reshape(512, 128), prolong_matrix(128, 96, 256, 192)).reshape(16, 32, 256)

        def rows(i, carry):
            mid = 0.75 * es0[i, 4:28, :]
            even = (mid + 0.25 * es0[i, 3:27, :]) * ke[...]
            odd = (mid + 0.25 * es0[i, 5:29, :]) * ko[...]
            ye0[i] = even
            yo0[i] = odd
            return carry

        lax.fori_loop(first, 16 - first, rows, 0)

        def planes(k, carry):
            for x, pair_of in enumerate(plane_pair(ye0, yo0, 1, k)):
                i = 2 * k + x
                for y, value in enumerate(pair_of):
                    value = value * in_x(i)
                    for h in range(2):
                        at_rows = (h, i, pl.ds(y, 24, 2))
                        part = value[:, 128 * h : 128 * h + 128]
                        v1[at_rows] = v1[at_rows] + part if add else part
            return carry

        lax.fori_loop(first, 14 - first, planes, 0)

    atoms = atom_copies()
    start(atoms)
    rho_copies = copies1(0, SEM_RHO, (0, 1))
    start(rho_copies)
    v_copies = copies0(vf, 0, SEM_V, (0, 6))
    start(v_copies)

    for ref in (v1, g1, f3, e3, f4, v4, a2, w3):
        ref[...] = jnp.zeros(ref.shape, F32)
    k0[...] = grid_mask((1, 48, 256), (0, 32 * gy - 8, 128 * gz), (128, 256, 1024), 192, (-8, 136))[0]
    y_even = 2 * iota((24, 256), 0) + 32 * gy - 8
    z_at = wrapped(iota((24, 256), 1), 192, 256)
    z_in = (z_at >= -8) & (z_at < 136) & (z_at + 128 * gz >= 0) & (z_at + 128 * gz < 1024)
    y_in = (y_even >= 0) & (y_even < 256)
    ke[...] = jnp.where(y_in & z_in, 1.0, 0.0)
    ko[...] = ke[...]
    k1[...] = grid_mask((16, 32, 128), (8 * gx - 4, 16 * gy - 8, 64 * gz), (64, 128, 512), 96, (-8, 72))
    k2[...] = grid_mask((12, 24, 128), (4 * gx - 4, 8 * gy - 8, 32 * gz), (32, 64, 256), 96, (-32, 64))
    k3[...] = grid_mask((10, 24, 128), (2 * gx - 4, 4 * gy - 8, 16 * gz), (16, 32, 128), 64, (-16, 32))
    kg[...] = grid_mask((4, 16, 128), (2 * gx - 1, 4 * gy - 4, 16 * gz), (16, 32, 128), 64, (-16, 32))
    k4[...] = grid_mask((8, 32, 128), (0, -8, 8 * gz), (8, 16, 64), 64, (-8, 16))

    wait_send(rho_copies)
    wait_recv(rho_copies)
    unpack1(0)
    prolong0(f1[0], 3, False)

    wait_recv(atoms)
    by_atom = at[...]
    by_param = by_atom.T

    def factor(coord, centre, low):
        u = (coord - centre) * 0.5
        e = jnp.where((coord >= low) & (coord < low + 12.0), jnp.exp(-u * u), 0.0)
        return u, e

    def row(k):
        return by_param[k : k + 1, :]

    def coordinates(shape, dim, first):
        return (iota(shape, dim) + first).astype(F32)

    ux, ex = factor(coordinates((16, 128), 0, 16 * gx), row(10), row(13))
    uy, ey = factor(coordinates((32, 128), 0, 32 * gy), row(11), row(14))
    uz, ez = factor(coordinates((128, 128), 1, 128 * gz), by_atom[:, 12:13], by_atom[:, 15:16])
    uex = ux * ex
    p00 = row(0) * ex + row(1) * uex + row(7) * (ux * uex)
    p01 = row(2) * ex + row(4) * uex
    p02 = row(8) * ex
    p10 = row(3) * ex + row(6) * uex
    p11 = row(5) * ex
    p20 = row(9) * ex
    uey = uy * ey
    uuey = uy * uey
    for x in range(16):
        s = slice(x, x + 1)
        pln[32 * x : 32 * x + 32, 0:128] = p00[s] * ey + p01[s] * uey + p02[s] * uuey
        pln[32 * x : 32 * x + 32, 128:256] = p10[s] * ey + p11[s] * uey
        pln[32 * x : 32 * x + 32, 256:384] = p20[s] * ey
    uez = uz * ez
    z_hi, z_lo = split(jnp.concatenate([ez, uez, uz * uez], axis=0))
    p_hi, p_lo = split(pln[...])
    block = dot(p_hi, z_hi) + dot(p_hi, z_lo) + dot(p_lo, z_hi)
    block = block.reshape(16, 32, 128) + v1[0, 6:22, 8:40, :]
    dens[...] = block
    ff[6:22, 8:40, 0:128] = block

    pack0(ff, 1)
    f_copies = copies0(ff, 1, SEM_F, (0, 3))
    start(f_copies)
    late = late_copies()
    start(late)
    wait_send(v_copies)
    wait_recv(v_copies)
    unpack0(vf, 0, (*range(6), *range(22, 28)), True)
    wait_recv(f_copies)
    unpack0(ff, 1, (3, 4, 5, 22, 23, 24), True)

    def cycle(q, carry):
        base = SEM_CYCLE + q * PER_CYCLE
        c1 = copies1(q + 1, base, (0, 4))
        c2 = copies2(q, base + N_DIR)
        c4a = copies4a(q, base + 2 * N_DIR)
        c4b = copies4b(q, base + 2 * N_DIR + N_RING)
        c3a = copies3a(q, base + 2 * N_DIR + 2 * N_RING)
        c3b = copies3b(q, base + 2 * N_DIR + 2 * N_RING + len(X_NEAR))

        def pre(k, carry):
            values = []
            for i in (2 * k + 1, 2 * k + 2):
                c = vf[i]
                value = 0.2 * c + ALPHA * (ff[i] + spread(c, vf[i - 1], vf[i + 1]))
                values.append((i, value * (k0[...] * in_x(i))))
            for i, value in values:
                v1[0, i] = value[:, 0:128]
                v1[1, i] = value[:, 128:256]
            return carry

        lax.fori_loop(1, 12, pre, 0)

        def residual(k, carry):
            total = None
            for i in (2 * k + 4, 2 * k + 5):
                c = both(v1, i)
                r = ff[i] - 6.0 * c + spread(c, both(v1, i - 1), both(v1, i + 1))
                total = r if total is None else total + r
            s0[0] = total[:, 0:128]
            s0[1] = total[:, 128:256]
            a0[k] = jnp.concatenate([halve_rows(s0.at[h], 0, 24) for h in range(2)], axis=1)
            return carry

        lax.fori_loop(0, 10, residual, 0)
        g = 0.125 * mm(a0[...].reshape(240, 256), restrict_matrix(256, 192, 128, 96))
        g1[:, 4:28, :] = g.reshape(10, 24, 128)
        g1[...] = g1[...] * k1[3:13]
        f1[q + 1, 4:12, 8:24, :] = g1[1:9, 8:24, :]

        c, nb = neighbours(g1, 1, 8)
        r = (0.2 * c + ALPHA * nb).reshape(4, 2, 32, 128)
        s1[...] = r[:, 0] + r[:, 1]
        parts = jnp.concatenate(
            [s1[x, pl.ds(8, 8, 2), :] + s1[x, pl.ds(9, 8, 2), :] for x in range(4)], axis=1
        )
        row_at = iota((512, 128), 0)
        col_at = iota((512, 128), 1)
        lane_at = row_at & 127
        m2 = jnp.where((lane_at < 64) & ((row_at >> 7) * 32 + (lane_at >> 1) == col_at), 1.0, 0.0).astype(BF16)
        t2[q, 1, 1, 8:16] = 0.125 * mm(parts, m2)
        start(c2)
        pack1(q + 1)
        start(c1)

        wait_recv(c2)
        unpack2(q)
        c, nb = neighbours(f2, 2, 8)
        r = (0.2 * c + ALPHA * nb).reshape(4, 2, 24, 128)
        s2[...] = r[:, 0] + r[:, 1]
        a2[:, 0:12, :] = s2[:, pl.ds(0, 12, 2), :] + s2[:, pl.ds(1, 12, 2), :]
        g = 0.125 * mm(a2[...].reshape(64, 128), restrict_matrix(128, 96, 128, 64))
        g3[...] = g.reshape(4, 16, 128) * kg[...]
        c, nb = neighbours(g3, 1, 2)
        r = 0.2 * c + ALPHA * nb
        s4[...] = r[0] + r[1]
        parts = jnp.concatenate([s4[4:5] + s4[5:6], s4[6:7] + s4[7:8]], axis=1)
        row_at = iota((256, 128), 0)
        z_at = wrapped(row_at & 127, 64, 128) >> 1
        live = (z_at >= -8) & (z_at < 16) & (z_at + 8 * gz >= 0) & (z_at + 8 * gz < 64)
        m4 = jnp.where(live & (32 * (row_at >> 7) + z_at + 8 == iota((256, 128), 1)), 1.0, 0.0).astype(BF16)
        xa[q, gx] = 0.125 * mm(jnp.broadcast_to(parts, (8, 256)), m4)[0:1]
        start(c4a)
        tile = jnp.concatenate([g3[1, 4:8, :], g3[2, 4:8, :]], axis=0)
        x1[q, 0] = pltpu.roll(jnp.where(iota((8, 128), 1) < 16, tile, 0.0), 16 * gx, 1)
        start(c3a)
        wait_send(c2)
        wait_send(c1)
        wait_recv(c1)
        unpack1(q + 1)
        wait_recv(c4a)
        yb[q, gy] = xa[q].reshape(8, 128)
        start(c4b)
        wait_recv(c3a)
        total = x1[q, 0]
        for n in range(len(X_NEAR)):
            total = total + x1[q, n + 1]
        y1[q, 1, 8:16] = total
        start(c3b)
        wait_send(c4a)
        wait_send(c3a)

        @pl.when(q == 0)
        def _():
            wait_send(f_copies)
            wait_send(late)
            wait_recv(late)
            unpack0(ff, 1, (1, 2, 25, 26), False)
            pre(0, 0)
            pre(12, 0)

        wait_recv(c3b)
        unpack3(q)
        wait_recv(c4b)
        unpack4(q)

        weight4, weight3, weight2, weight1 = (ALPHA * 4.0**level for level in (4, 3, 2, 1))
        v4[4:12] = weight4 * f4[...]
        for _ in range(3):
            c, nb = neighbours(v4, 4, 8)
            v4[4:12] = (0.2 * c + ALPHA * nb + weight4 * f4[...]) * k4[...]

        near = v4[pl.ds(gx + 1, 7)].reshape(224, 128)
        es3[...] = mm(near, prolong_matrix(128, 64, 128, 64)).reshape(7, 32, 128)
        expand_rows(es3, ye3, yo3, 2 * gy + 4, 12)
        for k in range(5):
            expand_planes(ye3, yo3, w3, 0, 1, k)
        rhs = weight3 * f3[...]
        e3[...] = (rhs + w3[...]) * k3[...]
        c, nb = neighbours(e3, 1, 8)
        e3[1:9] = (0.2 * c + ALPHA * nb + rhs[1:9]) * k3[1:9]

        near = e3[1:9].reshape(192, 128)
        es2[...] = mm(near, prolong_matrix(128, 64, 128, 96)).reshape(8, 24, 128)
        expand_rows(es2, ye2, yo2, 4, 12)
        for k in range(6):
            expand_planes(ye2, yo2, w2, 0, 1, k)
        rhs = weight2 * f2[...]
        e2[...] = (rhs + w2[...]) * k2[...]
        c, nb = neighbours(e2, 1, 10)
        e2[1:11] = (0.2 * c + ALPHA * nb + rhs[1:11]) * k2[1:11]

        es1[...] = mm(e2[...].reshape(288, 128), prolong_matrix(128, 96, 128, 96)).reshape(12, 24, 128)
        expand_rows(es1, ye1, yo1, 4, 16)
        for k in range(8):
            expand_planes(ye1, yo1, w1, 0, 2, k)
        rhs = weight1 * f1[q + 1]
        e1[...] = (rhs + w1[...]) * k1[...]
        c, nb = neighbours(e1, 1, 14)
        e1[1:15] = (0.2 * c + ALPHA * nb + rhs[1:15]) * k1[1:15]

        prolong0(e1[...], 2 * q, True)

        def post(k, carry):
            values = []
            for i in (2 * k + 2, 2 * k + 3):
                c = both(v1, i)
                value = 0.2 * c + ALPHA * (ff[i] + spread(c, both(v1, i - 1), both(v1, i + 1)))
                values.append((i, value * (k0[...] * in_x(i))))
            for i, value in values:
                vf[i] = value
            return carry

        lax.fori_loop(2 * q, 12 - 2 * q, post, 0)
        wait_send(c4b)
        wait_send(c3b)
        return carry

    lax.fori_loop(0, 2, cycle, 0)
    pot[...] = vf[6:22, 8:40, 0:128]
    wait_send(atoms)


def scratch():
    def vm(*shape):
        return pltpu.VMEM(shape, F32)

    return [
        vm(28, 48, 256), vm(2, 28, 48, 128), vm(28, 48, 256),
        vm(2, 3, 48, 128), vm(2, 3, 48, 128), vm(2, 2, 32, 128), vm(8, 16, 64),
        vm(3, 16, 32, 128), vm(3, 3, 32, 128), vm(3, 3, 32, 128), vm(3, 16, 128),
        vm(10, 32, 128), vm(10, 24, 256), vm(2, 48, 128), vm(16, 32, 256), vm(16, 24, 256), vm(16, 24, 256),
        vm(16, 32, 128), vm(16, 32, 128), vm(12, 24, 128), vm(12, 16, 128), vm(12, 16, 128),
        vm(2, 3, 3, 24, 128), vm(12, 24, 128), vm(12, 24, 128), vm(12, 24, 128), vm(4, 32, 128),
        vm(8, 24, 128), vm(8, 12, 128), vm(8, 12, 128),
        vm(2, 5, 8, 128), vm(2, 3, 24, 128), vm(10, 24, 128), vm(10, 24, 128), vm(10, 24, 128),
        vm(4, 24, 128), vm(4, 16, 128), vm(4, 16, 128), vm(16, 128), vm(7, 32, 128), vm(7, 12, 128), vm(7, 12, 128),
        vm(2, 8, 1, 128), vm(2, 8, 8, 128), vm(2, 64, 128), vm(8, 32, 128), vm(16, 32, 128),
        vm(128, 128), vm(128, 128), vm(512, 384),
        vm(48, 256), vm(24, 256), vm(24, 256),
        vm(16, 32, 128), vm(12, 24, 128), vm(10, 24, 128), vm(4, 16, 128), vm(8, 32, 128),
        pltpu.SemaphoreType.DMA((2,)), pltpu.SemaphoreType.DMA((N_SEMS,)), pltpu.SemaphoreType.DMA((N_SEMS,)),
    ]


def per_device(coarse_density, start_potential, pair_density, expansion, box_corners, box_offsets, lists, counts):
    del lists, counts
    block = jax.ShapeDtypeStruct((16, 32, 128), F32)
    vmem = pl.BlockSpec(memory_space=pltpu.VMEM)
    hbm = pl.BlockSpec(memory_space=pltpu.HBM)
    return pl.pallas_call(
        kernel,
        out_shape=(block, block),
        in_specs=[hbm] * 2 + [vmem] * 4,
        out_specs=(vmem, vmem),
        scratch_shapes=scratch(),
        compiler_params=pltpu.CompilerParams(
            collective_id=0, has_side_effects=True, vmem_limit_bytes=40 * 2**20
        ),
    )(coarse_density, start_potential, pair_density, expansion.T, box_corners.T, box_offsets.T)


def solution(mesh):
    everywhere = P(AXES, None)
    in_specs = (P(*AXES), P(*AXES), everywhere, P(), everywhere, everywhere, everywhere, P(AXES))
    return jax.shard_map(
        per_device, mesh=mesh, in_specs=in_specs, out_specs=(P(*AXES), P(*AXES)), check_vma=False
    )
```

```python
import itertools

import jax
import jax.numpy as jnp
from jax import lax
from jax.experimental import pallas as pl
from jax.experimental.pallas import tpu as pltpu
from jax.sharding import PartitionSpec as P

F32 = jnp.float32
BF16 = jnp.bfloat16
MESH = pl.DeviceIdType.MESH
ALPHA = 0.8 / 6.0
AXES = ("gx", "gy", "gz")
DIRS = [d for d in itertools.product((-1, 0, 1), repeat=3) if d != (0, 0, 0)]
DIRS.sort(key=lambda d: -sum(map(abs, d)))
XY_DIRS = [d for d in DIRS if d[2] == 0 and d[0] != 0]
UP7 = [d for d in itertools.product((0, 1), repeat=3) if d != (0, 0, 0)]
RING = [4, 3, 5, 2, 6, 1, 7]
X_NEAR = [1, -1, 2, -2]
YZ_NEAR = [d for d in DIRS if d[0] == 0]
N_ATOM, N_DIR, N_RING = len(UP7), len(DIRS), len(RING)
SEM_V = N_ATOM
SEM_RHO = SEM_V + N_DIR
SEM_F = SEM_RHO + N_DIR
SEM_LATE = SEM_F + N_DIR
SEM_CYCLE = SEM_LATE + len(XY_DIRS)
PER_CYCLE = 2 * N_DIR + 2 * N_RING + len(X_NEAR) + len(YZ_NEAR)
N_SEMS = SEM_CYCLE + 2 * PER_CYCLE


def iota(shape, dim):
    return lax.broadcasted_iota(jnp.int32, shape, dim)


def wrapped(lane, cut, lanes):
    return jnp.where(lane < cut, lane, lane - lanes)


def split(a):
    hi = a.astype(BF16)
    return hi, (a - hi.astype(F32)).astype(BF16)


def dot(a, b):
    return jnp.dot(a, b, preferred_element_type=F32)


def mm(a, m):
    hi, lo = split(a)
    return dot(hi, m) + dot(lo, m)


def restrict_matrix(rows, rcut, cols, ccut):
    fine = wrapped(iota((rows, cols), 0), rcut, rows)
    coarse = wrapped(iota((rows, cols), 1), ccut, cols)
    return jnp.where((fine >> 1) == coarse, 1.0, 0.0).astype(BF16)


def prolong_matrix(rows, rcut, cols, ccut):
    coarse = wrapped(iota((rows, cols), 0), rcut, rows)
    fine = wrapped(iota((rows, cols), 1), ccut, cols)
    centre = fine >> 1
    other = jnp.where((fine & 1) == 0, centre - 1, centre + 1)
    return jnp.where(coarse == centre, 0.75, jnp.where(coarse == other, 0.25, 0.0)).astype(BF16)


def grid_mask(shape, starts, sizes, cut, window):
    x = iota(shape, 0) + starts[0]
    y = iota(shape, 1) + starts[1]
    z = wrapped(iota(shape, 2), cut, shape[2])
    near = (z >= window[0]) & (z < window[1])
    z = z + starts[2]
    inside = (x >= 0) & (x < sizes[0]) & (y >= 0) & (y < sizes[1]) & (z >= 0) & (z < sizes[2])
    return jnp.where(inside & near, 1.0, 0.0)


def neighbours(ref, first, count):
    c = ref[pl.ds(first, count)]
    rows, lanes = c.shape[1], c.shape[2]
    total = ref[pl.ds(first - 1, count)] + ref[pl.ds(first + 1, count)]
    total = total + pltpu.roll(c, 1, 1) + pltpu.roll(c, rows - 1, 1)
    return c, total + pltpu.roll(c, 1, 2) + pltpu.roll(c, lanes - 1, 2)


def expand_rows(es, ye, yo, r0, nr):
    def rows(start):
        return es[:, pl.ds(start, nr), :]

    mid = 0.75 * rows(r0)
    ye[...] = mid + 0.25 * rows(r0 - 1)
    yo[...] = mid + 0.25 * rows(r0 + 1)


def plane_pair(ye, yo, c0, k):
    pairs = []
    e, o = 0.75 * ye[k + c0], 0.75 * yo[k + c0]
    for side in (k + c0 - 1, k + c0 + 1):
        pairs.append((e + 0.25 * ye[side], o + 0.25 * yo[side]))
    return pairs


def expand_planes(ye, yo, out, f0, c0, k):
    for x, (even, odd) in enumerate(plane_pair(ye, yo, c0, k)):
        n = even.shape[0]
        out[f0 + 2 * k + x, pl.ds(0, n, 2), :] = even
        out[f0 + 2 * k + x, pl.ds(1, n, 2), :] = odd


def both(ref, i):
    return jnp.concatenate([ref[0, i], ref[1, i]], axis=1)


def spread(c, before, after):
    rows, lanes = c.shape
    total = before + after + pltpu.roll(c, 1, 0) + pltpu.roll(c, rows - 1, 0)
    return total + pltpu.roll(c, 1, 1) + pltpu.roll(c, lanes - 1, 1)


def halve_rows(ref, start, count):
    return ref[pl.ds(start, count, 2), :] + ref[pl.ds(start + 1, count, 2), :]


def kernel(
    rho_hbm, v0_hbm, pair_hbm, expn_hbm, corner_hbm, offset_hbm, dens, pot,
    pair, expn_t, corner_t, offset_t, vf, v1, ff, zl0, zh0, zs0, rho,
    f1, zl1, zh1, zs1, g1, a0, s0, es0, ye0, yo0, e1, w1, es1, ye1, yo1,
    t2, f2, e2, w2, s1, es2, ye2, yo2,
    x1, y1, f3, e3, w3, s2, a2, g3, s4, es3, ye3, yo3,
    xa, yb, ts, f4, v4,
    at, tp, pln, k0, ke, ko, k1, k2, k3, kg, k4, local, ss, rs,
):
    gx, gy, gz = (lax.axis_index(a) for a in AXES)
    here = (gx, gy, gz)

    def peer(d):
        return tuple(i if s == 0 else lax.rem(i + (s + 8), 8) for i, s in zip(here, d))

    rho_in = pltpu.make_async_copy(rho_hbm, rho, local.at[0])
    v0_in = pltpu.make_async_copy(v0_hbm, vf.at[6:22, 8:40, 0:128], local.at[1])
    small_in = [
        pltpu.make_async_copy(src, dst, local.at[2 + k])
        for k, (src, dst) in enumerate(
            ((pair_hbm, pair), (expn_hbm, expn_t), (corner_hbm, corner_t), (offset_hbm, offset_t))
        )
    ]
    for item in [rho_in, v0_in] + small_in:
        item.start()
    barrier = pltpu.get_barrier_semaphore()
    reached = []
    for d in DIRS[::-1] + [(k, 0, 0) for k in RING] + [(0, k, 0) for k in RING]:
        d = tuple(s % 8 for s in d)
        if d not in reached:
            reached.append(d)
    for d in reached:
        pl.semaphore_signal(barrier, inc=1, device_id=peer(d), device_id_type=MESH)

    def pack0(frame, q):
        lane = iota((32, 128), 1)
        lo = hi = jnp.zeros((32, 128), F32)
        for x in range(16):
            t = frame[6 + x, 8:40, 0:128]
            if x:
                t = pltpu.roll(t, 8 * x, 1)
            h = (8 * x - 8) % 128
            lo = jnp.where((lane >= 8 * x) & (lane < 8 * x + 8), t, lo)
            hi = jnp.where((lane >= h) & (lane < h + 8), t, hi)
        zs0[q, 0] = lo
        zs0[q, 1] = hi

    def pack1(q):
        lane = iota((16, 128), 1)
        out = jnp.zeros((16, 128), F32)
        for x in range(8):
            t = f1[q, 4 + x, 8:24, :]
            lo = t if x == 0 else pltpu.roll(t, 16 * x, 1)
            hi = t if x == 3 else pltpu.roll(t, (16 * x - 48) % 128, 1)
            out = jnp.where((lane >= 16 * x) & (lane < 16 * x + 8), lo, out)
            out = jnp.where((lane >= 16 * x + 8) & (lane < 16 * x + 16), hi, out)
        zs1[q] = out

    hi_prec = lax.Precision.HIGHEST
    m = iota((9, 128), 0)
    c = iota((9, 128), 1)
    one = jnp.where((c < 7) & (m == c), 1.0, 0.0)
    one = one + jnp.where((c == 7) & (m == 7), 1.0, 0.0) - jnp.where((c == 7) & (m == 8), 1.0, 0.0)
    one = one - jnp.where((c == 8) & (m >= 7), 1.0, 0.0) + jnp.where((c == 9) & (m == 8), 2.0, 0.0)
    for item in small_in:
        item.wait()
    moments = lax.dot_general(
        pair[...], expn_t[...], (((1,), (1,)), ((), ())), precision=hi_prec, preferred_element_type=F32
    )
    packed = jnp.dot(moments, one, precision=hi_prec)
    corners = corner_t[...].astype(F32)
    tp[...] = jnp.zeros(tp.shape, F32)
    tp[10:13, 0:16] = corners + 5.5 + offset_t[...]
    tp[13:16, 0:16] = corners
    at[0:16, :] = packed + tp[...].T[0:16]
    rho_in.wait()
    f1[0, 4:12, 8:24, 0:64] = rho[...]
    pack1(0)
    v0_in.wait()
    pack0(vf, 0)

    pl.semaphore_wait(barrier, len(reached))

    def rcopy(src, dst, k, d):
        return pltpu.make_async_remote_copy(
            src_ref=src, dst_ref=dst, send_sem=ss.at[k], recv_sem=rs.at[k], device_id=peer(d), device_id_type=MESH
        )

    def atom_copies():
        return [
            rcopy(at.at[0:16], at.at[16 * k + 16 : 16 * k + 32], k, d) for k, d in enumerate(UP7)
        ]

    def frame_slices(d, nx, hx, ny, part):
        near, far = part
        src, dst = [], []
        for s, n, h, o, a, b in ((d[0], nx, hx, hx, near, far), (d[1], ny, 8, 8, 0, 8)):
            if s == 0:
                src.append(slice(o, o + n))
                dst.append(slice(o, o + n))
            elif s > 0:
                src.append(slice(o + n - b, o + n - a))
                dst.append(slice(h - b, h - a))
            else:
                src.append(slice(o + a, o + b))
                dst.append(slice(o + n + a, o + n + b))
        return tuple(src), tuple(dst)

    def copies0(frame, q, base, part):
        out = []
        for k, d in enumerate(DIRS):
            src, dst = frame_slices(d, 16, 6, 32, part)
            if d[2] == 0:
                out.append(rcopy(frame.at[src + (slice(0, 128),)], frame.at[dst + (slice(0, 128),)], base + k, d))
            else:
                rows = slice(src[1].start - 8, src[1].stop - 8)
                zr = zh0 if d[2] > 0 else zl0
                out.append(rcopy(zs0.at[q, 1 if d[2] > 0 else 0, rows], zr.at[q, 1 - d[0], dst[1]], base + k, d))
        return out

    def late_copies():
        out = []
        for k, d in enumerate(XY_DIRS):
            src, dst = frame_slices(d, 16, 6, 32, (3, 5))
            out.append(rcopy(ff.at[src + (slice(0, 128),)], ff.at[dst + (slice(0, 128),)], SEM_LATE + k, d))
        return out

    def copies1(q, base, part):
        out = []
        for k, d in enumerate(DIRS):
            src, dst = frame_slices(d, 8, 4, 16, part)
            if d[2] == 0:
                out.append(rcopy(f1.at[(q,) + src], f1.at[(q,) + dst], base + k, d))
            else:
                rows = slice(src[1].start - 8, src[1].stop - 8)
                zr = zh1 if d[2] > 0 else zl1
                out.append(rcopy(zs1.at[q, rows], zr.at[q, 1 - d[0], dst[1]], base + k, d))
        return out

    def copies2(q, base):
        mine = t2.at[q, 1, 1, 8:16]
        return [
            rcopy(mine, t2.at[q, 1 - d[2], 1 - d[0], 8 * (1 - d[1]) : 8 * (1 - d[1]) + 8], base + k, d)
            for k, d in enumerate(DIRS)
        ]

    def copies3a(q, base):
        return [rcopy(x1.at[q, 0], x1.at[q, k + 1], base + k, (n, 0, 0)) for k, n in enumerate(X_NEAR)]

    def copies3b(q, base):
        return [
            rcopy(y1.at[q, 1, 8:16], y1.at[q, 1 - d[2], 8 * (1 - d[1]) : 8 * (1 - d[1]) + 8], base + k, d)
            for k, d in enumerate(YZ_NEAR)
        ]

    def copies4a(q, base):
        return [rcopy(xa.at[q, gx], xa.at[q, gx], base + k, (n, 0, 0)) for k, n in enumerate(RING)]

    def copies4b(q, base):
        return [rcopy(yb.at[q, gy], yb.at[q, gy], base + k, (0, n, 0)) for k, n in enumerate(RING)]

    def start(copies):
        for item in copies:
            item.start()

    def wait_recv(copies):
        for item in copies:
            item.wait_recv()

    def wait_send(copies):
        for item in copies:
            item.wait_send()

    def in_x(i):
        x = 16 * gx + i - 6
        return jnp.where((x >= 0) & (x < 128), 1.0, 0.0)

    def unpack0(frame, q, halo, own):
        lane = iota((48, 128), 1)
        keep = (lane < 8) | (lane >= 120)

        def beside(slot, sx, i):
            t = jnp.where((lane >= 8 * sx) & (lane < 8 * sx + 8), zl0[q, slot], zh0[q, slot])
            t = pltpu.roll(t, lax.rem(128 - 8 * sx, 128), 1)
            return jnp.where(keep, t, 0.0) * (k0[:, 128:256] * in_x(i))

        for i in halo:
            below = i < 6
            frame[i, :, 0:128] = frame[i, :, 0:128] * (k0[:, 0:128] * in_x(i))
            frame[i, :, 128:256] = beside(0 if below else 2, jnp.int32(i + 10 if below else i - 22), i)

        def body(k, carry):
            values = [(i, beside(1, i - 6, i)) for i in (2 * k + 6, 2 * k + 7)]
            for i, value in values:
                frame[i, :, 128:256] = value
                for rows in (slice(0, 8), slice(40, 48)):
                    frame[i, rows, 0:128] = frame[i, rows, 0:128] * k0[rows, 0:128]
            return carry

        if own:
            lax.fori_loop(0, 8, body, 0)

    def unpack1(q):
        lane = iota((32, 128), 1)
        for i in range(16) if not isinstance(q, int) else range(3, 13):
            slot = 0 if i < 4 else 1 if i < 12 else 2
            sx = (4 + i) % 8 if i < 4 else (i - 4) % 8
            lo = zl1[q, slot]
            hi = zh1[q, slot]
            if (64 - 16 * sx) % 128:
                lo = pltpu.roll(lo, (64 - 16 * sx) % 128, 1)
            if (112 - 16 * sx) % 128:
                hi = pltpu.roll(hi, (112 - 16 * sx) % 128, 1)
            t = jnp.where(lane < 64, f1[q, i], jnp.where(lane < 72, lo, jnp.where(lane >= 120, hi, 0.0)))
            f1[q, i] = t * k1[i]

    def unpack2(q):
        lane = iota((24, 128), 1)
        for i in range(12):
            slot, sx = i // 4, i % 4
            below, mid, above = t2[q, 0, slot], t2[q, 1, slot], t2[q, 2, slot]
            if sx:
                mid = pltpu.roll(mid, 128 - 32 * sx, 1)
            if sx != 1:
                above = pltpu.roll(above, (32 - 32 * sx) % 128, 1)
            if sx != 3:
                below = pltpu.roll(below, 96 - 32 * sx, 1)
            t = jnp.where(lane < 32, mid, jnp.where(lane < 64, above, jnp.where(lane >= 96, below, 0.0)))
            f2[i] = t * k2[i]

    def unpack3(q):
        lane = iota((24, 128), 1)
        for dx in range(-2, 3):
            shift = 16 * lax.rem(gx + (dx + 8), 8)

            def turned(slot, target):
                return pltpu.roll(y1[q, slot], lax.rem(128 + target - shift, 128), 1)

            t = jnp.where(lane < 16, turned(1, 0), 0.0)
            t = jnp.where((lane >= 16) & (lane < 32), turned(2, 16), t)
            t = jnp.where(lane >= 112, turned(0, 112), t)
            for y in range(3):
                for x in range(2):
                    f3[2 * dx + 4 + x, 4 + 4 * y : 8 + 4 * y, :] = t[8 * y + 4 * x : 8 * y + 4 * x + 4]
        f3[...] = f3[...] * k3[...]

    def unpack4(q):
        lane = iota((64, 128), 1)
        for y in range(2):
            t = pltpu.roll(yb[q].reshape(64, 128), 120 - 32 * y, 1)
            ts[y] = jnp.where((lane < 16) | (lane >= 120), t, 0.0)
        for x in range(8):
            for y in range(2):
                f4[x, pl.ds(8 + y, 8, 2), :] = ts[y, pl.ds(x, 8, 8), :]

    def prolong0(source, first, add):
        es0[...] = mm(source.reshape(512, 128), prolong_matrix(128, 96, 256, 192)).reshape(16, 32, 256)

        def rows(i, carry):
            mid = 0.75 * es0[i, 4:28, :]
            even = (mid + 0.25 * es0[i, 3:27, :]) * ke[...]
            odd = (mid + 0.25 * es0[i, 5:29, :]) * ko[...]
            ye0[i] = even
            yo0[i] = odd
            return carry

        lax.fori_loop(first, 16 - first, rows, 0)

        def planes(k, carry):
            for x, pair_of in enumerate(plane_pair(ye0, yo0, 1, k)):
                i = 2 * k + x
                for y, value in enumerate(pair_of):
                    value = value * in_x(i)
                    for h in range(2):
                        at_rows = (h, i, pl.ds(y, 24, 2))
                        part = value[:, 128 * h : 128 * h + 128]
                        v1[at_rows] = v1[at_rows] + part if add else part
            return carry

        lax.fori_loop(first, 14 - first, planes, 0)

    atoms = atom_copies()
    start(atoms)
    rho_copies = copies1(0, SEM_RHO, (0, 1))
    start(rho_copies)
    v_copies = copies0(vf, 0, SEM_V, (0, 6))
    start(v_copies)

    for ref in (v1, g1, f3, e3, f4, v4, a2, w3):
        ref[...] = jnp.zeros(ref.shape, F32)
    k0[...] = grid_mask((1, 48, 256), (0, 32 * gy - 8, 128 * gz), (128, 256, 1024), 192, (-8, 136))[0]
    y_even = 2 * iota((24, 256), 0) + 32 * gy - 8
    z_at = wrapped(iota((24, 256), 1), 192, 256)
    z_in = (z_at >= -8) & (z_at < 136) & (z_at + 128 * gz >= 0) & (z_at + 128 * gz < 1024)
    y_in = (y_even >= 0) & (y_even < 256)
    ke[...] = jnp.where(y_in & z_in, 1.0, 0.0)
    ko[...] = ke[...]
    k1[...] = grid_mask((16, 32, 128), (8 * gx - 4, 16 * gy - 8, 64 * gz), (64, 128, 512), 96, (-8, 72))
    k2[...] = grid_mask((12, 24, 128), (4 * gx - 4, 8 * gy - 8, 32 * gz), (32, 64, 256), 96, (-32, 64))
    k3[...] = grid_mask((10, 24, 128), (2 * gx - 4, 4 * gy - 8, 16 * gz), (16, 32, 128), 64, (-16, 32))
    kg[...] = grid_mask((4, 16, 128), (2 * gx - 1, 4 * gy - 4, 16 * gz), (16, 32, 128), 64, (-16, 32))
    k4[...] = grid_mask((8, 32, 128), (0, -8, 8 * gz), (8, 16, 64), 64, (-8, 16))

    wait_send(rho_copies)
    wait_recv(rho_copies)
    unpack1(0)
    prolong0(f1[0], 3, False)

    wait_recv(atoms)
    by_atom = at[...]
    by_param = by_atom.T

    def factor(coord, centre, low):
        u = (coord - centre) * 0.5
        e = jnp.where((coord >= low) & (coord < low + 12.0), jnp.exp(-u * u), 0.0)
        return u, e

    def row(k):
        return by_param[k : k + 1, :]

    def coordinates(shape, dim, first):
        return (iota(shape, dim) + first).astype(F32)

    ux, ex = factor(coordinates((16, 128), 0, 16 * gx), row(10), row(13))
    uy, ey = factor(coordinates((32, 128), 0, 32 * gy), row(11), row(14))
    uz, ez = factor(coordinates((128, 128), 1, 128 * gz), by_atom[:, 12:13], by_atom[:, 15:16])
    uex = ux * ex
    p00 = row(0) * ex + row(1) * uex + row(7) * (ux * uex)
    p01 = row(2) * ex + row(4) * uex
    p02 = row(8) * ex
    p10 = row(3) * ex + row(6) * uex
    p11 = row(5) * ex
    p20 = row(9) * ex
    uey = uy * ey
    uuey = uy * uey
    for x in range(16):
        s = slice(x, x + 1)
        pln[32 * x : 32 * x + 32, 0:128] = p00[s] * ey + p01[s] * uey + p02[s] * uuey
        pln[32 * x : 32 * x + 32, 128:256] = p10[s] * ey + p11[s] * uey
        pln[32 * x : 32 * x + 32, 256:384] = p20[s] * ey
    uez = uz * ez
    z_hi, z_lo = split(jnp.concatenate([ez, uez, uz * uez], axis=0))
    p_hi, p_lo = split(pln[...])
    block = dot(p_hi, z_hi) + dot(p_hi, z_lo) + dot(p_lo, z_hi)
    block = block.reshape(16, 32, 128) + v1[0, 6:22, 8:40, :]
    dens[...] = block
    ff[6:22, 8:40, 0:128] = block

    pack0(ff, 1)
    f_copies = copies0(ff, 1, SEM_F, (0, 3))
    start(f_copies)
    late = late_copies()
    start(late)
    wait_send(v_copies)
    wait_recv(v_copies)
    unpack0(vf, 0, (*range(6), *range(22, 28)), True)
    wait_recv(f_copies)
    unpack0(ff, 1, (3, 4, 5, 22, 23, 24), True)

    def cycle(q, carry):
        base = SEM_CYCLE + q * PER_CYCLE
        c1 = copies1(q + 1, base, (0, 4))
        c2 = copies2(q, base + N_DIR)
        c4a = copies4a(q, base + 2 * N_DIR)
        c4b = copies4b(q, base + 2 * N_DIR + N_RING)
        c3a = copies3a(q, base + 2 * N_DIR + 2 * N_RING)
        c3b = copies3b(q, base + 2 * N_DIR + 2 * N_RING + len(X_NEAR))

        def pre(first, count):
            values = []
            for i in [first + j for j in range(count)]:
                c = vf[i]
                value = 0.2 * c + ALPHA * (ff[i] + spread(c, vf[i - 1], vf[i + 1]))
                values.append((i, value * (k0[...] * in_x(i))))
            for i, value in values:
                v1[0, i] = value[:, 0:128]
                v1[1, i] = value[:, 128:256]

        @pl.loop(0, 2)
        def _(k):
            pre(11 * k + 3, 11)

        @pl.loop(0, 5)
        def _(k):
            sums = []
            for pair_at in (2 * k, 2 * k + 1):
                total = None
                for i in (2 * pair_at + 4, 2 * pair_at + 5):
                    c = both(v1, i)
                    r = ff[i] - 6.0 * c + spread(c, both(v1, i - 1), both(v1, i + 1))
                    total = r if total is None else total + r
                sums.append((pair_at, total))
            for n, (_, total) in enumerate(sums):
                s0[n, 0] = total[:, 0:128]
                s0[n, 1] = total[:, 128:256]
            for n, (pair_at, _) in enumerate(sums):
                a0[pair_at] = jnp.concatenate([halve_rows(s0.at[n, h], 0, 24) for h in range(2)], axis=1)

        g = 0.125 * mm(a0[...].reshape(240, 256), restrict_matrix(256, 192, 128, 96))
        g1[:, 4:28, :] = g.reshape(10, 24, 128)
        g1[...] = g1[...] * k1[3:13]
        f1[q + 1, 4:12, 8:24, :] = g1[1:9, 8:24, :]

        c, nb = neighbours(g1, 1, 8)
        r = (0.2 * c + ALPHA * nb).reshape(4, 2, 32, 128)
        s1[...] = r[:, 0] + r[:, 1]
        parts = jnp.concatenate(
            [s1[x, pl.ds(8, 8, 2), :] + s1[x, pl.ds(9, 8, 2), :] for x in range(4)], axis=1
        )
        row_at = iota((512, 128), 0)
        col_at = iota((512, 128), 1)
        lane_at = row_at & 127
        m2 = jnp.where((lane_at < 64) & ((row_at >> 7) * 32 + (lane_at >> 1) == col_at), 1.0, 0.0).astype(BF16)
        t2[q, 1, 1, 8:16] = 0.125 * mm(parts, m2)
        start(c2)
        pack1(q + 1)
        start(c1)

        wait_recv(c2)
        unpack2(q)
        c, nb = neighbours(f2, 2, 8)
        r = (0.2 * c + ALPHA * nb).reshape(4, 2, 24, 128)
        s2[...] = r[:, 0] + r[:, 1]
        a2[:, 0:12, :] = s2[:, pl.ds(0, 12, 2), :] + s2[:, pl.ds(1, 12, 2), :]
        g = 0.125 * mm(a2[...].reshape(64, 128), restrict_matrix(128, 96, 128, 64))
        g3[...] = g.reshape(4, 16, 128) * kg[...]
        c, nb = neighbours(g3, 1, 2)
        r = 0.2 * c + ALPHA * nb
        s4[...] = r[0] + r[1]
        parts = jnp.concatenate([s4[4:5] + s4[5:6], s4[6:7] + s4[7:8]], axis=1)
        row_at = iota((256, 128), 0)
        z_at = wrapped(row_at & 127, 64, 128) >> 1
        live = (z_at >= -8) & (z_at < 16) & (z_at + 8 * gz >= 0) & (z_at + 8 * gz < 64)
        m4 = jnp.where(live & (32 * (row_at >> 7) + z_at + 8 == iota((256, 128), 1)), 1.0, 0.0).astype(BF16)
        xa[q, gx] = 0.125 * mm(jnp.broadcast_to(parts, (8, 256)), m4)[0:1]
        start(c4a)
        tile = jnp.concatenate([g3[1, 4:8, :], g3[2, 4:8, :]], axis=0)
        x1[q, 0] = pltpu.roll(jnp.where(iota((8, 128), 1) < 16, tile, 0.0), 16 * gx, 1)
        start(c3a)
        wait_send(c2)
        wait_send(c1)
        wait_recv(c1)
        unpack1(q + 1)
        wait_recv(c4a)
        yb[q, gy] = xa[q].reshape(8, 128)
        start(c4b)
        wait_recv(c3a)
        total = x1[q, 0]
        for n in range(len(X_NEAR)):
            total = total + x1[q, n + 1]
        y1[q, 1, 8:16] = total
        start(c3b)
        wait_send(c4a)
        wait_send(c3a)

        @pl.when(q == 0)
        def _():
            wait_send(f_copies)
            wait_send(late)
            wait_recv(late)
            unpack0(ff, 1, (1, 2, 25, 26), False)
            pre(1, 2)
            pre(25, 2)

        wait_recv(c3b)
        unpack3(q)
        wait_recv(c4b)
        unpack4(q)

        weight4, weight3, weight2, weight1 = (ALPHA * 4.0**level for level in (4, 3, 2, 1))
        v4[4:12] = weight4 * f4[...]
        for _ in range(3):
            c, nb = neighbours(v4, 4, 8)
            v4[4:12] = (0.2 * c + ALPHA * nb + weight4 * f4[...]) * k4[...]

        near = v4[pl.ds(gx + 1, 7)].reshape(224, 128)
        es3[...] = mm(near, prolong_matrix(128, 64, 128, 64)).reshape(7, 32, 128)
        expand_rows(es3, ye3, yo3, 2 * gy + 4, 12)
        for k in range(5):
            expand_planes(ye3, yo3, w3, 0, 1, k)
        rhs = weight3 * f3[...]
        e3[...] = (rhs + w3[...]) * k3[...]
        c, nb = neighbours(e3, 1, 8)
        e3[1:9] = (0.2 * c + ALPHA * nb + rhs[1:9]) * k3[1:9]

        near = e3[1:9].reshape(192, 128)
        es2[...] = mm(near, prolong_matrix(128, 64, 128, 96)).reshape(8, 24, 128)
        expand_rows(es2, ye2, yo2, 4, 12)
        for k in range(6):
            expand_planes(ye2, yo2, w2, 0, 1, k)
        rhs = weight2 * f2[...]
        e2[...] = (rhs + w2[...]) * k2[...]
        c, nb = neighbours(e2, 1, 10)
        e2[1:11] = (0.2 * c + ALPHA * nb + rhs[1:11]) * k2[1:11]

        es1[...] = mm(e2[...].reshape(288, 128), prolong_matrix(128, 96, 128, 96)).reshape(12, 24, 128)
        expand_rows(es1, ye1, yo1, 4, 16)
        for k in range(8):
            expand_planes(ye1, yo1, w1, 0, 2, k)
        rhs = weight1 * f1[q + 1]
        e1[...] = (rhs + w1[...]) * k1[...]
        c, nb = neighbours(e1, 1, 14)
        e1[1:15] = (0.2 * c + ALPHA * nb + rhs[1:15]) * k1[1:15]

        prolong0(e1[...], 2 * q, True)

        def post(k, carry):
            values = []
            for i in [8 * k + 4 * q + 2 + j for j in range(8)]:
                c = both(v1, i)
                value = 0.2 * c + ALPHA * (ff[i] + spread(c, both(v1, i - 1), both(v1, i + 1)))
                values.append((i, value * (k0[...] * in_x(i))))
            for i, value in values:
                vf[i] = value
            return carry

        lax.fori_loop(0, 3 - q, post, 0)
        wait_send(c4b)
        wait_send(c3b)
        return carry

    lax.fori_loop(0, 2, cycle, 0)
    pot[...] = vf[6:22, 8:40, 0:128]
    wait_send(atoms)


def scratch():
    def vm(*shape):
        return pltpu.VMEM(shape, F32)

    return [
        vm(16, 91), vm(9, 91), pltpu.VMEM((3, 16), jnp.int32), vm(3, 16),
        vm(28, 48, 256), vm(2, 28, 48, 128), vm(28, 48, 256),
        vm(2, 3, 48, 128), vm(2, 3, 48, 128), vm(2, 2, 32, 128), vm(8, 16, 64),
        vm(3, 16, 32, 128), vm(3, 3, 32, 128), vm(3, 3, 32, 128), vm(3, 16, 128),
        vm(10, 32, 128), vm(10, 24, 256), vm(2, 2, 48, 128), vm(16, 32, 256), vm(16, 24, 256), vm(16, 24, 256),
        vm(16, 32, 128), vm(16, 32, 128), vm(12, 24, 128), vm(12, 16, 128), vm(12, 16, 128),
        vm(2, 3, 3, 24, 128), vm(12, 24, 128), vm(12, 24, 128), vm(12, 24, 128), vm(4, 32, 128),
        vm(8, 24, 128), vm(8, 12, 128), vm(8, 12, 128),
        vm(2, 5, 8, 128), vm(2, 3, 24, 128), vm(10, 24, 128), vm(10, 24, 128), vm(10, 24, 128),
        vm(4, 24, 128), vm(4, 16, 128), vm(4, 16, 128), vm(16, 128), vm(7, 32, 128), vm(7, 12, 128), vm(7, 12, 128),
        vm(2, 8, 1, 128), vm(2, 8, 8, 128), vm(2, 64, 128), vm(8, 32, 128), vm(16, 32, 128),
        vm(128, 128), vm(128, 128), vm(512, 384),
        vm(48, 256), vm(24, 256), vm(24, 256),
        vm(16, 32, 128), vm(12, 24, 128), vm(10, 24, 128), vm(4, 16, 128), vm(8, 32, 128),
        pltpu.SemaphoreType.DMA((6,)), pltpu.SemaphoreType.DMA((N_SEMS,)), pltpu.SemaphoreType.DMA((N_SEMS,)),
    ]


def per_device(coarse_density, start_potential, pair_density, expansion, box_corners, box_offsets, lists, counts):
    del lists, counts
    block = jax.ShapeDtypeStruct((16, 32, 128), F32)
    vmem = pl.BlockSpec(memory_space=pltpu.VMEM)
    hbm = pl.BlockSpec(memory_space=pltpu.HBM)
    return pl.pallas_call(
        kernel,
        out_shape=(block, block),
        in_specs=[hbm] * 6,
        out_specs=(vmem, vmem),
        scratch_shapes=scratch(),
        compiler_params=pltpu.CompilerParams(
            collective_id=0, has_side_effects=True, vmem_limit_bytes=64 * 2**20
        ),
    )(coarse_density, start_potential, pair_density, expansion.T, box_corners.T, box_offsets.T)


def solution(mesh):
    everywhere = P(AXES, None)
    in_specs = (P(*AXES), P(*AXES), everywhere, P(), everywhere, everywhere, everywhere, P(AXES))
    return jax.shard_map(
        per_device, mesh=mesh, in_specs=in_specs, out_specs=(P(*AXES), P(*AXES)), check_vma=False
    )
```

```python
import itertools

import jax
import jax.numpy as jnp
from jax import lax
from jax.experimental import pallas as pl
from jax.experimental.pallas import tpu as pltpu
from jax.sharding import PartitionSpec as P

F32 = jnp.float32
BF16 = jnp.bfloat16
MESH = pl.DeviceIdType.MESH
ALPHA = 0.8 / 6.0
AXES = ("gx", "gy", "gz")
DIRS = [d for d in itertools.product((-1, 0, 1), repeat=3) if d != (0, 0, 0)]
DIRS.sort(key=lambda d: -sum(map(abs, d)))
XY_DIRS = [d for d in DIRS if d[2] == 0 and d[0] != 0]
UP7 = [d for d in itertools.product((0, 1), repeat=3) if d != (0, 0, 0)]
RING = [4, 3, 5, 2, 6, 1, 7]
X_NEAR = [1, -1, 2, -2]
YZ_NEAR = [d for d in DIRS if d[0] == 0]
N_ATOM, N_DIR, N_RING = len(UP7), len(DIRS), len(RING)
SEM_V = N_ATOM
SEM_RHO = SEM_V + N_DIR
SEM_F = SEM_RHO + N_DIR
SEM_LATE = SEM_F + N_DIR
SEM_CYCLE = SEM_LATE + len(XY_DIRS)
PER_CYCLE = 2 * N_DIR + 2 * N_RING + len(X_NEAR) + len(YZ_NEAR)
N_SEMS = SEM_CYCLE + 2 * PER_CYCLE


def iota(shape, dim):
    return lax.broadcasted_iota(jnp.int32, shape, dim)


def wrapped(lane, cut, lanes):
    return jnp.where(lane < cut, lane, lane - lanes)


def split(a):
    hi = a.astype(BF16)
    return hi, (a - hi.astype(F32)).astype(BF16)


def dot(a, b):
    return jnp.dot(a, b, preferred_element_type=F32)


def mm(a, m):
    hi, lo = split(a)
    return dot(hi, m) + dot(lo, m)


def restrict_matrix(rows, rcut, cols, ccut):
    fine = wrapped(iota((rows, cols), 0), rcut, rows)
    coarse = wrapped(iota((rows, cols), 1), ccut, cols)
    return jnp.where((fine >> 1) == coarse, 1.0, 0.0).astype(BF16)


def prolong_matrix(rows, rcut, cols, ccut):
    coarse = wrapped(iota((rows, cols), 0), rcut, rows)
    fine = wrapped(iota((rows, cols), 1), ccut, cols)
    centre = fine >> 1
    other = jnp.where((fine & 1) == 0, centre - 1, centre + 1)
    return jnp.where(coarse == centre, 0.75, jnp.where(coarse == other, 0.25, 0.0)).astype(BF16)


def grid_mask(shape, starts, sizes, cut, window):
    x = iota(shape, 0) + starts[0]
    y = iota(shape, 1) + starts[1]
    z = wrapped(iota(shape, 2), cut, shape[2])
    near = (z >= window[0]) & (z < window[1])
    z = z + starts[2]
    inside = (x >= 0) & (x < sizes[0]) & (y >= 0) & (y < sizes[1]) & (z >= 0) & (z < sizes[2])
    return jnp.where(inside & near, 1.0, 0.0)


def neighbours(ref, first, count):
    c = ref[pl.ds(first, count)]
    rows, lanes = c.shape[1], c.shape[2]
    total = ref[pl.ds(first - 1, count)] + ref[pl.ds(first + 1, count)]
    total = total + pltpu.roll(c, 1, 1) + pltpu.roll(c, rows - 1, 1)
    return c, total + pltpu.roll(c, 1, 2) + pltpu.roll(c, lanes - 1, 2)


def expand_rows(es, ye, yo, r0, nr):
    def rows(start):
        return es[:, pl.ds(start, nr), :]

    mid = 0.75 * rows(r0)
    ye[...] = mid + 0.25 * rows(r0 - 1)
    yo[...] = mid + 0.25 * rows(r0 + 1)


def plane_pair(ye, yo, c0, k):
    pairs = []
    e, o = 0.75 * ye[k + c0], 0.75 * yo[k + c0]
    for side in (k + c0 - 1, k + c0 + 1):
        pairs.append((e + 0.25 * ye[side], o + 0.25 * yo[side]))
    return pairs


def expand_planes(ye, yo, out, f0, c0, k):
    for x, (even, odd) in enumerate(plane_pair(ye, yo, c0, k)):
        n = even.shape[0]
        out[f0 + 2 * k + x, pl.ds(0, n, 2), :] = even
        out[f0 + 2 * k + x, pl.ds(1, n, 2), :] = odd


def both(ref, i):
    return jnp.concatenate([ref[0, i], ref[1, i]], axis=1)


def spread(c, before, after):
    rows, lanes = c.shape
    total = before + after + pltpu.roll(c, 1, 0) + pltpu.roll(c, rows - 1, 0)
    return total + pltpu.roll(c, 1, 1) + pltpu.roll(c, lanes - 1, 1)


def halve_rows(ref, start, count):
    return ref[pl.ds(start, count, 2), :] + ref[pl.ds(start + 1, count, 2), :]


def kernel(
    rho_hbm, v0_hbm, pair_hbm, expn_hbm, corner_hbm, offset_hbm, smooth_out, local_out, sweep_out,
    smooth, gauss, pair, expn_t, corner_t, offset_t, vf, v1, ff, zl0, zh0, zs0, rho,
    f1, zl1, zh1, zs1, g1, a0, s0, es0, ye0, yo0, e1, w1, es1, ye1, yo1,
    t2, f2, e2, w2, s1, es2, ye2, yo2,
    x1, y1, f3, e3, w3, s2, a2, g3, s4, es3, ye3, yo3,
    xa, yb, ts, f4, v4,
    at, tp, pln, k0, ke, ko, k1, k2, k3, kg, k4, local, ss, rs,
):
    gx, gy, gz = (lax.axis_index(a) for a in AXES)
    here = (gx, gy, gz)

    def peer(d):
        return tuple(i if s == 0 else lax.rem(i + (s + 8), 8) for i, s in zip(here, d))

    rho_in = pltpu.make_async_copy(rho_hbm, rho, local.at[0])
    v0_in = pltpu.make_async_copy(v0_hbm, vf.at[6:22, 8:40, 0:128], local.at[1])
    small_in = [
        pltpu.make_async_copy(src, dst, local.at[2 + k])
        for k, (src, dst) in enumerate(
            ((pair_hbm, pair), (expn_hbm, expn_t), (corner_hbm, corner_t), (offset_hbm, offset_t))
        )
    ]
    for item in [rho_in, v0_in] + small_in:
        item.start()
    barrier = pltpu.get_barrier_semaphore()
    reached = []
    for d in DIRS[::-1] + [(k, 0, 0) for k in RING] + [(0, k, 0) for k in RING]:
        d = tuple(s % 8 for s in d)
        if d not in reached:
            reached.append(d)
    for d in reached:
        pl.semaphore_signal(barrier, inc=1, device_id=peer(d), device_id_type=MESH)

    def pack0(frame, q):
        lane = iota((32, 128), 1)
        lo = hi = jnp.zeros((32, 128), F32)
        for x in range(16):
            t = frame[6 + x, 8:40, 0:128]
            if x:
                t = pltpu.roll(t, 8 * x, 1)
            h = (8 * x - 8) % 128
            lo = jnp.where((lane >= 8 * x) & (lane < 8 * x + 8), t, lo)
            hi = jnp.where((lane >= h) & (lane < h + 8), t, hi)
        zs0[q, 0] = lo
        zs0[q, 1] = hi

    def pack1(q):
        lane = iota((16, 128), 1)
        out = jnp.zeros((16, 128), F32)
        for x in range(8):
            t = f1[q, 4 + x, 8:24, :]
            lo = t if x == 0 else pltpu.roll(t, 16 * x, 1)
            hi = t if x == 3 else pltpu.roll(t, (16 * x - 48) % 128, 1)
            out = jnp.where((lane >= 16 * x) & (lane < 16 * x + 8), lo, out)
            out = jnp.where((lane >= 16 * x + 8) & (lane < 16 * x + 16), hi, out)
        zs1[q] = out

    hi_prec = lax.Precision.HIGHEST
    m = iota((9, 128), 0)
    c = iota((9, 128), 1)
    one = jnp.where((c < 7) & (m == c), 1.0, 0.0)
    one = one + jnp.where((c == 7) & (m == 7), 1.0, 0.0) - jnp.where((c == 7) & (m == 8), 1.0, 0.0)
    one = one - jnp.where((c == 8) & (m >= 7), 1.0, 0.0) + jnp.where((c == 9) & (m == 8), 2.0, 0.0)
    for item in small_in:
        item.wait()
    moments = lax.dot_general(
        pair[...], expn_t[...], (((1,), (1,)), ((), ())), precision=hi_prec, preferred_element_type=F32
    )
    packed = jnp.dot(moments, one, precision=hi_prec)
    corners = corner_t[...].astype(F32)
    tp[...] = jnp.zeros(tp.shape, F32)
    tp[10:13, 0:16] = corners + 5.5 + offset_t[...]
    tp[13:16, 0:16] = corners
    at[0:16, :] = packed + tp[...].T[0:16]
    rho_in.wait()
    f1[0, 4:12, 8:24, 0:64] = rho[...]
    pack1(0)
    v0_in.wait()
    pack0(vf, 0)

    pl.semaphore_wait(barrier, len(reached))

    def rcopy(src, dst, k, d):
        return pltpu.make_async_remote_copy(
            src_ref=src, dst_ref=dst, send_sem=ss.at[k], recv_sem=rs.at[k], device_id=peer(d), device_id_type=MESH
        )

    def atom_copies():
        return [
            rcopy(at.at[0:16], at.at[16 * k + 16 : 16 * k + 32], k, d) for k, d in enumerate(UP7)
        ]

    def frame_slices(d, nx, hx, ny, part):
        near, far = part
        src, dst = [], []
        for s, n, h, o, a, b in ((d[0], nx, hx, hx, near, far), (d[1], ny, 8, 8, 0, 8)):
            if s == 0:
                src.append(slice(o, o + n))
                dst.append(slice(o, o + n))
            elif s > 0:
                src.append(slice(o + n - b, o + n - a))
                dst.append(slice(h - b, h - a))
            else:
                src.append(slice(o + a, o + b))
                dst.append(slice(o + n + a, o + n + b))
        return tuple(src), tuple(dst)

    def copies0(frame, q, base, part):
        out = []
        for k, d in enumerate(DIRS):
            src, dst = frame_slices(d, 16, 6, 32, part)
            if d[2] == 0:
                out.append(rcopy(frame.at[src + (slice(0, 128),)], frame.at[dst + (slice(0, 128),)], base + k, d))
            else:
                rows = slice(src[1].start - 8, src[1].stop - 8)
                zr = zh0 if d[2] > 0 else zl0
                out.append(rcopy(zs0.at[q, 1 if d[2] > 0 else 0, rows], zr.at[q, 1 - d[0], dst[1]], base + k, d))
        return out

    def late_copies():
        out = []
        for k, d in enumerate(XY_DIRS):
            src, dst = frame_slices(d, 16, 6, 32, (3, 5))
            out.append(rcopy(ff.at[src + (slice(0, 128),)], ff.at[dst + (slice(0, 128),)], SEM_LATE + k, d))
        return out

    def copies1(q, base, part):
        out = []
        for k, d in enumerate(DIRS):
            src, dst = frame_slices(d, 8, 4, 16, part)
            if d[2] == 0:
                out.append(rcopy(f1.at[(q,) + src], f1.at[(q,) + dst], base + k, d))
            else:
                rows = slice(src[1].start - 8, src[1].stop - 8)
                zr = zh1 if d[2] > 0 else zl1
                out.append(rcopy(zs1.at[q, rows], zr.at[q, 1 - d[0], dst[1]], base + k, d))
        return out

    def copies2(q, base):
        mine = t2.at[q, 1, 1, 8:16]
        return [
            rcopy(mine, t2.at[q, 1 - d[2], 1 - d[0], 8 * (1 - d[1]) : 8 * (1 - d[1]) + 8], base + k, d)
            for k, d in enumerate(DIRS)
        ]

    def copies3a(q, base):
        return [rcopy(x1.at[q, 0], x1.at[q, k + 1], base + k, (n, 0, 0)) for k, n in enumerate(X_NEAR)]

    def copies3b(q, base):
        return [
            rcopy(y1.at[q, 1, 8:16], y1.at[q, 1 - d[2], 8 * (1 - d[1]) : 8 * (1 - d[1]) + 8], base + k, d)
            for k, d in enumerate(YZ_NEAR)
        ]

    def copies4a(q, base):
        return [rcopy(xa.at[q, gx], xa.at[q, gx], base + k, (n, 0, 0)) for k, n in enumerate(RING)]

    def copies4b(q, base):
        return [rcopy(yb.at[q, gy], yb.at[q, gy], base + k, (0, n, 0)) for k, n in enumerate(RING)]

    def start(copies):
        for item in copies:
            item.start()

    def wait_recv(copies):
        for item in copies:
            item.wait_recv()

    def wait_send(copies):
        for item in copies:
            item.wait_send()

    def in_x(i):
        x = 16 * gx + i - 6
        return jnp.where((x >= 0) & (x < 128), 1.0, 0.0)

    def unpack0(frame, q, halo, own):
        lane = iota((48, 128), 1)
        keep = (lane < 8) | (lane >= 120)

        def beside(slot, sx, i):
            t = jnp.where((lane >= 8 * sx) & (lane < 8 * sx + 8), zl0[q, slot], zh0[q, slot])
            t = pltpu.roll(t, lax.rem(128 - 8 * sx, 128), 1)
            return jnp.where(keep, t, 0.0) * (k0[:, 128:256] * in_x(i))

        for i in halo:
            below = i < 6
            frame[i, :, 0:128] = frame[i, :, 0:128] * (k0[:, 0:128] * in_x(i))
            frame[i, :, 128:256] = beside(0 if below else 2, jnp.int32(i + 10 if below else i - 22), i)

        def body(k, carry):
            values = [(i, beside(1, i - 6, i)) for i in [4 * k + 6 + j for j in range(4)]]
            for i, value in values:
                frame[i, :, 128:256] = value
                for rows in (slice(0, 8), slice(40, 48)):
                    frame[i, rows, 0:128] = frame[i, rows, 0:128] * k0[rows, 0:128]
            return carry

        if own:
            lax.fori_loop(0, 4, body, 0)

    def unpack1(q):
        lane = iota((32, 128), 1)
        for i in range(16) if not isinstance(q, int) else range(3, 13):
            slot = 0 if i < 4 else 1 if i < 12 else 2
            sx = (4 + i) % 8 if i < 4 else (i - 4) % 8
            lo = zl1[q, slot]
            hi = zh1[q, slot]
            if (64 - 16 * sx) % 128:
                lo = pltpu.roll(lo, (64 - 16 * sx) % 128, 1)
            if (112 - 16 * sx) % 128:
                hi = pltpu.roll(hi, (112 - 16 * sx) % 128, 1)
            t = jnp.where(lane < 64, f1[q, i], jnp.where(lane < 72, lo, jnp.where(lane >= 120, hi, 0.0)))
            f1[q, i] = t * k1[i]

    def unpack2(q):
        lane = iota((24, 128), 1)
        for i in range(12):
            slot, sx = i // 4, i % 4
            below, mid, above = t2[q, 0, slot], t2[q, 1, slot], t2[q, 2, slot]
            if sx:
                mid = pltpu.roll(mid, 128 - 32 * sx, 1)
            if sx != 1:
                above = pltpu.roll(above, (32 - 32 * sx) % 128, 1)
            if sx != 3:
                below = pltpu.roll(below, 96 - 32 * sx, 1)
            t = jnp.where(lane < 32, mid, jnp.where(lane < 64, above, jnp.where(lane >= 96, below, 0.0)))
            f2[i] = t * k2[i]

    def unpack3(q):
        lane = iota((24, 128), 1)
        for dx in range(-2, 3):
            shift = 16 * lax.rem(gx + (dx + 8), 8)

            def turned(slot, target):
                return pltpu.roll(y1[q, slot], lax.rem(128 + target - shift, 128), 1)

            t = jnp.where(lane < 16, turned(1, 0), 0.0)
            t = jnp.where((lane >= 16) & (lane < 32), turned(2, 16), t)
            t = jnp.where(lane >= 112, turned(0, 112), t)
            for y in range(3):
                for x in range(2):
                    f3[2 * dx + 4 + x, 4 + 4 * y : 8 + 4 * y, :] = t[8 * y + 4 * x : 8 * y + 4 * x + 4]
        f3[...] = f3[...] * k3[...]

    def unpack4(q):
        lane = iota((64, 128), 1)
        for y in range(2):
            t = pltpu.roll(yb[q].reshape(64, 128), 120 - 32 * y, 1)
            ts[y] = jnp.where((lane < 16) | (lane >= 120), t, 0.0)
        for x in range(8):
            for y in range(2):
                f4[x, pl.ds(8 + y, 8, 2), :] = ts[y, pl.ds(x, 8, 8), :]

    def prolong0(source, first, add):
        es0[...] = mm(source.reshape(512, 128), prolong_matrix(128, 96, 256, 192)).reshape(16, 32, 256)

        def rows(k, carry):
            values = []
            for i in (first + 2 * k, first + 2 * k + 1):
                mid = 0.75 * es0[i, 4:28, :]
                even = (mid + 0.25 * es0[i, 3:27, :]) * ke[...]
                odd = (mid + 0.25 * es0[i, 5:29, :]) * ko[...]
                values.append((i, even, odd))
            for i, even, odd in values:
                ye0[i] = even
                yo0[i] = odd
            return carry

        lax.fori_loop(0, 8 - first, rows, 0)

        def planes(step, carry):
            for k in (first + 2 * step, first + 2 * step + 1):
                for x, pair_of in enumerate(plane_pair(ye0, yo0, 1, k)):
                    i = 2 * k + x
                    for y, value in enumerate(pair_of):
                        value = value * in_x(i)
                        for h in range(2):
                            at_rows = (h, i, pl.ds(y, 24, 2))
                            part = value[:, 128 * h : 128 * h + 128]
                            v1[at_rows] = v1[at_rows] + part if add else part
            return carry

        lax.fori_loop(0, 7 - first, planes, 0)

    atoms = atom_copies()
    start(atoms)
    rho_copies = copies1(0, SEM_RHO, (0, 1))
    start(rho_copies)
    v_copies = copies0(vf, 0, SEM_V, (0, 6))
    start(v_copies)

    for ref in (v1, g1, f3, e3, f4, v4, a2, w3):
        ref[...] = jnp.zeros(ref.shape, F32)
    k0[...] = grid_mask((1, 48, 256), (0, 32 * gy - 8, 128 * gz), (128, 256, 1024), 192, (-8, 136))[0]
    y_even = 2 * iota((24, 256), 0) + 32 * gy - 8
    z_at = wrapped(iota((24, 256), 1), 192, 256)
    z_in = (z_at >= -8) & (z_at < 136) & (z_at + 128 * gz >= 0) & (z_at + 128 * gz < 1024)
    y_in = (y_even >= 0) & (y_even < 256)
    ke[...] = jnp.where(y_in & z_in, 1.0, 0.0)
    ko[...] = ke[...]
    k1[...] = grid_mask((16, 32, 128), (8 * gx - 4, 16 * gy - 8, 64 * gz), (64, 128, 512), 96, (-8, 72))
    k2[...] = grid_mask((12, 24, 128), (4 * gx - 4, 8 * gy - 8, 32 * gz), (32, 64, 256), 96, (-32, 64))
    k3[...] = grid_mask((10, 24, 128), (2 * gx - 4, 4 * gy - 8, 16 * gz), (16, 32, 128), 64, (-16, 32))
    kg[...] = grid_mask((4, 16, 128), (2 * gx - 1, 4 * gy - 4, 16 * gz), (16, 32, 128), 64, (-16, 32))
    k4[...] = grid_mask((8, 32, 128), (0, -8, 8 * gz), (8, 16, 64), 64, (-8, 16))

    wait_send(rho_copies)
    wait_recv(rho_copies)
    unpack1(0)
    prolong0(f1[0], 3, False)

    wait_recv(atoms)
    by_atom = at[...]
    by_param = by_atom.T

    def factor(coord, centre, low):
        u = (coord - centre) * 0.5
        e = jnp.where((coord >= low) & (coord < low + 12.0), jnp.exp(-u * u), 0.0)
        return u, e

    def row(k):
        return by_param[k : k + 1, :]

    def coordinates(shape, dim, first):
        return (iota(shape, dim) + first).astype(F32)

    ux, ex = factor(coordinates((16, 128), 0, 16 * gx), row(10), row(13))
    uy, ey = factor(coordinates((32, 128), 0, 32 * gy), row(11), row(14))
    uz, ez = factor(coordinates((128, 128), 1, 128 * gz), by_atom[:, 12:13], by_atom[:, 15:16])
    uex = ux * ex
    p00 = row(0) * ex + row(1) * uex + row(7) * (ux * uex)
    p01 = row(2) * ex + row(4) * uex
    p02 = row(8) * ex
    p10 = row(3) * ex + row(6) * uex
    p11 = row(5) * ex
    p20 = row(9) * ex
    uey = uy * ey
    uuey = uy * uey
    for x in range(16):
        s = slice(x, x + 1)
        pln[32 * x : 32 * x + 32, 0:128] = p00[s] * ey + p01[s] * uey + p02[s] * uuey
        pln[32 * x : 32 * x + 32, 128:256] = p10[s] * ey + p11[s] * uey
        pln[32 * x : 32 * x + 32, 256:384] = p20[s] * ey
    uez = uz * ez
    z_hi, z_lo = split(jnp.concatenate([ez, uez, uz * uez], axis=0))
    p_hi, p_lo = split(pln[...])
    block = dot(p_hi, z_hi) + dot(p_hi, z_lo) + dot(p_lo, z_hi)
    gauss[...] = block.reshape(16, 32, 128)
    smooth[...] = v1[0, 6:22, 8:40, :]
    ff[6:22, 8:40, 0:128] = smooth[...] + gauss[...]
    parts_out = [
        pltpu.make_async_copy(smooth, smooth_out, local.at[6]),
        pltpu.make_async_copy(gauss, local_out, local.at[7]),
    ]

    pack0(ff, 1)
    f_copies = copies0(ff, 1, SEM_F, (0, 3))
    start(f_copies)
    late = late_copies()
    start(late)
    start(parts_out)
    wait_send(v_copies)
    wait_recv(v_copies)
    unpack0(vf, 0, (*range(6), *range(22, 28)), True)
    wait_recv(f_copies)
    unpack0(ff, 1, (3, 4, 5, 22, 23, 24), True)

    def cycle(q, carry):
        base = SEM_CYCLE + q * PER_CYCLE
        c1 = copies1(q + 1, base, (0, 4))
        c2 = copies2(q, base + N_DIR)
        c4a = copies4a(q, base + 2 * N_DIR)
        c4b = copies4b(q, base + 2 * N_DIR + N_RING)
        c3a = copies3a(q, base + 2 * N_DIR + 2 * N_RING)
        c3b = copies3b(q, base + 2 * N_DIR + 2 * N_RING + len(X_NEAR))

        def pre(first, count):
            values = []
            for i in [first + j for j in range(count)]:
                c = vf[i]
                value = 0.2 * c + ALPHA * (ff[i] + spread(c, vf[i - 1], vf[i + 1]))
                values.append((i, value * (k0[...] * in_x(i))))
            for i, value in values:
                v1[0, i] = value[:, 0:128]
                v1[1, i] = value[:, 128:256]

        @pl.loop(0, 2)
        def _(k):
            pre(11 * k + 3, 11)

        @pl.loop(0, 5)
        def _(k):
            sums = []
            for pair_at in (2 * k, 2 * k + 1):
                total = None
                for i in (2 * pair_at + 4, 2 * pair_at + 5):
                    c = both(v1, i)
                    r = ff[i] - 6.0 * c + spread(c, both(v1, i - 1), both(v1, i + 1))
                    total = r if total is None else total + r
                sums.append((pair_at, total))
            for n, (_, total) in enumerate(sums):
                s0[n, 0] = total[:, 0:128]
                s0[n, 1] = total[:, 128:256]
            for n, (pair_at, _) in enumerate(sums):
                a0[pair_at] = jnp.concatenate([halve_rows(s0.at[n, h], 0, 24) for h in range(2)], axis=1)

        g = 0.125 * mm(a0[...].reshape(240, 256), restrict_matrix(256, 192, 128, 96))
        g1[:, 4:28, :] = g.reshape(10, 24, 128)
        g1[...] = g1[...] * k1[3:13]
        f1[q + 1, 4:12, 8:24, :] = g1[1:9, 8:24, :]

        c, nb = neighbours(g1, 1, 8)
        r = (0.2 * c + ALPHA * nb).reshape(4, 2, 32, 128)
        s1[...] = r[:, 0] + r[:, 1]
        parts = jnp.concatenate(
            [s1[x, pl.ds(8, 8, 2), :] + s1[x, pl.ds(9, 8, 2), :] for x in range(4)], axis=1
        )
        row_at = iota((512, 128), 0)
        col_at = iota((512, 128), 1)
        lane_at = row_at & 127
        m2 = jnp.where((lane_at < 64) & ((row_at >> 7) * 32 + (lane_at >> 1) == col_at), 1.0, 0.0).astype(BF16)
        t2[q, 1, 1, 8:16] = 0.125 * mm(parts, m2)
        start(c2)
        pack1(q + 1)
        start(c1)

        wait_recv(c2)
        unpack2(q)
        c, nb = neighbours(f2, 2, 8)
        r = (0.2 * c + ALPHA * nb).reshape(4, 2, 24, 128)
        s2[...] = r[:, 0] + r[:, 1]
        a2[:, 0:12, :] = s2[:, pl.ds(0, 12, 2), :] + s2[:, pl.ds(1, 12, 2), :]
        g = 0.125 * mm(a2[...].reshape(64, 128), restrict_matrix(128, 96, 128, 64))
        g3[...] = g.reshape(4, 16, 128) * kg[...]
        c, nb = neighbours(g3, 1, 2)
        r = 0.2 * c + ALPHA * nb
        s4[...] = r[0] + r[1]
        parts = jnp.concatenate([s4[4:5] + s4[5:6], s4[6:7] + s4[7:8]], axis=1)
        row_at = iota((256, 128), 0)
        z_at = wrapped(row_at & 127, 64, 128) >> 1
        live = (z_at >= -8) & (z_at < 16) & (z_at + 8 * gz >= 0) & (z_at + 8 * gz < 64)
        m4 = jnp.where(live & (32 * (row_at >> 7) + z_at + 8 == iota((256, 128), 1)), 1.0, 0.0).astype(BF16)
        xa[q, gx] = 0.125 * mm(jnp.broadcast_to(parts, (8, 256)), m4)[0:1]
        start(c4a)
        tile = jnp.concatenate([g3[1, 4:8, :], g3[2, 4:8, :]], axis=0)
        x1[q, 0] = pltpu.roll(jnp.where(iota((8, 128), 1) < 16, tile, 0.0), 16 * gx, 1)
        start(c3a)
        wait_send(c2)
        wait_send(c1)
        wait_recv(c1)
        unpack1(q + 1)
        wait_recv(c4a)
        yb[q, gy] = xa[q].reshape(8, 128)
        start(c4b)
        wait_recv(c3a)
        total = x1[q, 0]
        for n in range(len(X_NEAR)):
            total = total + x1[q, n + 1]
        y1[q, 1, 8:16] = total
        start(c3b)
        wait_send(c4a)
        wait_send(c3a)

        @pl.when(q == 0)
        def _():
            wait_send(f_copies)
            wait_send(late)
            wait_recv(late)
            unpack0(ff, 1, (1, 2, 25, 26), False)
            pre(1, 2)
            pre(25, 2)

        wait_recv(c3b)
        unpack3(q)
        wait_recv(c4b)
        unpack4(q)

        weight4, weight3, weight2, weight1 = (ALPHA * 4.0**level for level in (4, 3, 2, 1))
        v4[4:12] = weight4 * f4[...]
        for _ in range(3):
            c, nb = neighbours(v4, 4, 8)
            v4[4:12] = (0.2 * c + ALPHA * nb + weight4 * f4[...]) * k4[...]

        near = v4[pl.ds(gx + 1, 7)].reshape(224, 128)
        es3[...] = mm(near, prolong_matrix(128, 64, 128, 64)).reshape(7, 32, 128)
        expand_rows(es3, ye3, yo3, 2 * gy + 4, 12)
        for k in range(5):
            expand_planes(ye3, yo3, w3, 0, 1, k)
        rhs = weight3 * f3[...]
        e3[...] = (rhs + w3[...]) * k3[...]
        c, nb = neighbours(e3, 1, 8)
        e3[1:9] = (0.2 * c + ALPHA * nb + rhs[1:9]) * k3[1:9]

        near = e3[1:9].reshape(192, 128)
        es2[...] = mm(near, prolong_matrix(128, 64, 128, 96)).reshape(8, 24, 128)
        expand_rows(es2, ye2, yo2, 4, 12)
        for k in range(6):
            expand_planes(ye2, yo2, w2, 0, 1, k)
        rhs = weight2 * f2[...]
        e2[...] = (rhs + w2[...]) * k2[...]
        c, nb = neighbours(e2, 1, 10)
        e2[1:11] = (0.2 * c + ALPHA * nb + rhs[1:11]) * k2[1:11]

        es1[...] = mm(e2[...].reshape(288, 128), prolong_matrix(128, 96, 128, 96)).reshape(12, 24, 128)
        expand_rows(es1, ye1, yo1, 4, 16)
        for k in range(8):
            expand_planes(ye1, yo1, w1, 0, 2, k)
        rhs = weight1 * f1[q + 1]
        e1[...] = (rhs + w1[...]) * k1[...]
        c, nb = neighbours(e1, 1, 14)
        e1[1:15] = (0.2 * c + ALPHA * nb + rhs[1:15]) * k1[1:15]

        prolong0(e1[...], 2 * q, True)

        source = jnp.where(q == 0, 1.0, 0.0)

        def post(k, carry):
            values = []
            for i in [8 * k + 4 * q + 2 + j for j in range(8)]:
                c = both(v1, i)
                value = 0.2 * c + ALPHA * (source * ff[i] + spread(c, both(v1, i - 1), both(v1, i + 1)))
                values.append((i, value * (k0[...] * in_x(i))))
            for i, value in values:
                vf[i] = value
            return carry

        lax.fori_loop(0, 3 - q, post, 0)
        wait_send(c4b)
        wait_send(c3b)
        return carry

    lax.fori_loop(0, 2, cycle, 0)
    result = pltpu.make_async_copy(vf.at[6:22, 8:40, 0:128], sweep_out, local.at[8])
    result.start()
    wait_send(atoms)
    for item in parts_out:
        item.wait()
    result.wait()


def scratch():
    def vm(*shape):
        return pltpu.VMEM(shape, F32)

    return [
        vm(16, 32, 128), vm(16, 32, 128), vm(16, 91), vm(9, 91), pltpu.VMEM((3, 16), jnp.int32), vm(3, 16),
        vm(28, 48, 256), vm(2, 28, 48, 128), vm(28, 48, 256),
        vm(2, 3, 48, 128), vm(2, 3, 48, 128), vm(2, 2, 32, 128), vm(8, 16, 64),
        vm(3, 16, 32, 128), vm(3, 3, 32, 128), vm(3, 3, 32, 128), vm(3, 16, 128),
        vm(10, 32, 128), vm(10, 24, 256), vm(2, 2, 48, 128), vm(16, 32, 256), vm(16, 24, 256), vm(16, 24, 256),
        vm(16, 32, 128), vm(16, 32, 128), vm(12, 24, 128), vm(12, 16, 128), vm(12, 16, 128),
        vm(2, 3, 3, 24, 128), vm(12, 24, 128), vm(12, 24, 128), vm(12, 24, 128), vm(4, 32, 128),
        vm(8, 24, 128), vm(8, 12, 128), vm(8, 12, 128),
        vm(2, 5, 8, 128), vm(2, 3, 24, 128), vm(10, 24, 128), vm(10, 24, 128), vm(10, 24, 128),
        vm(4, 24, 128), vm(4, 16, 128), vm(4, 16, 128), vm(16, 128), vm(7, 32, 128), vm(7, 12, 128), vm(7, 12, 128),
        vm(2, 8, 1, 128), vm(2, 8, 8, 128), vm(2, 64, 128), vm(8, 32, 128), vm(16, 32, 128),
        vm(128, 128), vm(128, 128), vm(512, 384),
        vm(48, 256), vm(24, 256), vm(24, 256),
        vm(16, 32, 128), vm(12, 24, 128), vm(10, 24, 128), vm(4, 16, 128), vm(8, 32, 128),
        pltpu.SemaphoreType.DMA((9,)), pltpu.SemaphoreType.DMA((N_SEMS,)), pltpu.SemaphoreType.DMA((N_SEMS,)),
    ]


def per_device(coarse_density, start_potential, pair_density, expansion, box_corners, box_offsets, lists, counts):
    del lists, counts
    block = jax.ShapeDtypeStruct((16, 32, 128), F32)
    hbm = pl.BlockSpec(memory_space=pltpu.HBM)
    smooth, gauss, sweep = pl.pallas_call(
        kernel,
        out_shape=(block, block, block),
        in_specs=[hbm] * 6,
        out_specs=(hbm, hbm, hbm),
        scratch_shapes=scratch(),
        compiler_params=pltpu.CompilerParams(
            collective_id=0, has_side_effects=True, vmem_limit_bytes=64 * 2**20
        ),
    )(coarse_density, start_potential, pair_density, expansion.T, box_corners.T, box_offsets.T)
    total_density = smooth + gauss
    return total_density, sweep + ALPHA * total_density


def solution(mesh):
    everywhere = P(AXES, None)
    in_specs = (P(*AXES), P(*AXES), everywhere, P(), everywhere, everywhere, everywhere, P(AXES))
    return jax.shard_map(
        per_device, mesh=mesh, in_specs=in_specs, out_specs=(P(*AXES), P(*AXES)), check_vma=False
    )
```

```python
import itertools

import jax
import jax.numpy as jnp
from jax import lax
from jax.experimental import pallas as pl
from jax.experimental.pallas import tpu as pltpu
from jax.sharding import PartitionSpec as P

F32 = jnp.float32
BF16 = jnp.bfloat16
MESH = pl.DeviceIdType.MESH
ALPHA = 0.8 / 6.0
AXES = ("gx", "gy", "gz")
DIRS = [d for d in itertools.product((-1, 0, 1), repeat=3) if d != (0, 0, 0)]
DIRS.sort(key=lambda d: -sum(map(abs, d)))
XY_DIRS = [d for d in DIRS if d[2] == 0 and d[0] != 0]
UP7 = [d for d in itertools.product((0, 1), repeat=3) if d != (0, 0, 0)]
RING = [4, 3, 5, 2, 6, 1, 7]
X_NEAR = [1, -1, 2, -2]
YZ_NEAR = [d for d in DIRS if d[0] == 0]
N_ATOM, N_DIR, N_RING = len(UP7), len(DIRS), len(RING)
SEM_V = N_ATOM
SEM_RHO = SEM_V + N_DIR
SEM_F = SEM_RHO + N_DIR
SEM_LATE = SEM_F + N_DIR
SEM_CYCLE = SEM_LATE + len(XY_DIRS)
PER_CYCLE = 2 * N_DIR + 2 * N_RING + len(X_NEAR) + len(YZ_NEAR)
N_SEMS = SEM_CYCLE + 2 * PER_CYCLE


def iota(shape, dim):
    return lax.broadcasted_iota(jnp.int32, shape, dim)


def wrapped(lane, cut, lanes):
    return jnp.where(lane < cut, lane, lane - lanes)


def split(a):
    hi = a.astype(BF16)
    return hi, (a - hi.astype(F32)).astype(BF16)


def dot(a, b):
    return jnp.dot(a, b, preferred_element_type=F32)


def mm(a, m):
    hi, lo = split(a)
    return dot(hi, m) + dot(lo, m)


def restrict_matrix(rows, rcut, cols, ccut):
    fine = wrapped(iota((rows, cols), 0), rcut, rows)
    coarse = wrapped(iota((rows, cols), 1), ccut, cols)
    return jnp.where((fine >> 1) == coarse, 1.0, 0.0).astype(BF16)


def prolong_matrix(rows, rcut, cols, ccut):
    coarse = wrapped(iota((rows, cols), 0), rcut, rows)
    fine = wrapped(iota((rows, cols), 1), ccut, cols)
    centre = fine >> 1
    other = jnp.where((fine & 1) == 0, centre - 1, centre + 1)
    return jnp.where(coarse == centre, 0.75, jnp.where(coarse == other, 0.25, 0.0)).astype(BF16)


def grid_mask(shape, starts, sizes, cut, window):
    x = iota(shape, 0) + starts[0]
    y = iota(shape, 1) + starts[1]
    z = wrapped(iota(shape, 2), cut, shape[2])
    near = (z >= window[0]) & (z < window[1])
    z = z + starts[2]
    inside = (x >= 0) & (x < sizes[0]) & (y >= 0) & (y < sizes[1]) & (z >= 0) & (z < sizes[2])
    return jnp.where(inside & near, 1.0, 0.0)


def neighbours(ref, first, count):
    c = ref[pl.ds(first, count)]
    rows, lanes = c.shape[1], c.shape[2]
    total = ref[pl.ds(first - 1, count)] + ref[pl.ds(first + 1, count)]
    total = total + pltpu.roll(c, 1, 1) + pltpu.roll(c, rows - 1, 1)
    return c, total + pltpu.roll(c, 1, 2) + pltpu.roll(c, lanes - 1, 2)


def expand_rows(es, ye, yo, r0, nr):
    def rows(start):
        return es[:, pl.ds(start, nr), :]

    mid = 0.75 * rows(r0)
    ye[...] = mid + 0.25 * rows(r0 - 1)
    yo[...] = mid + 0.25 * rows(r0 + 1)


def plane_pair(ye, yo, c0, k):
    pairs = []
    e, o = 0.75 * ye[k + c0], 0.75 * yo[k + c0]
    for side in (k + c0 - 1, k + c0 + 1):
        pairs.append((e + 0.25 * ye[side], o + 0.25 * yo[side]))
    return pairs


def expand_planes(ye, yo, out, f0, c0, k):
    for x, (even, odd) in enumerate(plane_pair(ye, yo, c0, k)):
        n = even.shape[0]
        out[f0 + 2 * k + x, pl.ds(0, n, 2), :] = even
        out[f0 + 2 * k + x, pl.ds(1, n, 2), :] = odd


def both(ref, i):
    return jnp.concatenate([ref[0, i], ref[1, i]], axis=1)


def spread(c, before, after):
    rows, lanes = c.shape
    total = before + after + pltpu.roll(c, 1, 0) + pltpu.roll(c, rows - 1, 0)
    return total + pltpu.roll(c, 1, 1) + pltpu.roll(c, lanes - 1, 1)


def halve_rows(ref, start, count):
    return ref[pl.ds(start, count, 2), :] + ref[pl.ds(start + 1, count, 2), :]


def kernel(
    rho_hbm, v0_hbm, pair_hbm, expn_hbm, corner_hbm, offset_hbm, smooth_out, local_out, sweep_out,
    smooth, gauss, pair, expn_t, corner_t, offset_t, vf, v1, ff, zl0, zh0, zs0, rho,
    f1, zl1, zh1, zs1, g1, a0, s0, es0, ye0, yo0, e1, w1, es1, ye1, yo1,
    t2, f2, e2, w2, s1, es2, ye2, yo2,
    x1, y1, f3, e3, w3, s2, a2, g3, s4, es3, ye3, yo3,
    xa, yb, ts, f4, v4,
    at, tp, pln, k0, ke, ko, k1, k2, k3, kg, k4, local, ss, rs,
):
    gx, gy, gz = (lax.axis_index(a) for a in AXES)
    here = (gx, gy, gz)

    def peer(d):
        return tuple(i if s == 0 else lax.rem(i + (s + 8), 8) for i, s in zip(here, d))

    rho_in = pltpu.make_async_copy(rho_hbm, rho, local.at[0])
    v0_in = pltpu.make_async_copy(v0_hbm, vf.at[6:22, 8:40, 0:128], local.at[1])
    small_in = [
        pltpu.make_async_copy(src, dst, local.at[2 + k])
        for k, (src, dst) in enumerate(
            ((pair_hbm, pair), (expn_hbm, expn_t), (corner_hbm, corner_t), (offset_hbm, offset_t))
        )
    ]
    for item in [rho_in, v0_in] + small_in:
        item.start()
    barrier = pltpu.get_barrier_semaphore()
    reached = []
    for d in DIRS[::-1] + [(k, 0, 0) for k in RING] + [(0, k, 0) for k in RING]:
        d = tuple(s % 8 for s in d)
        if d not in reached:
            reached.append(d)
    for d in reached:
        pl.semaphore_signal(barrier, inc=1, device_id=peer(d), device_id_type=MESH)

    def pack0(frame, q):
        lane = iota((32, 128), 1)
        lo = hi = jnp.zeros((32, 128), F32)
        for x in range(16):
            t = frame[6 + x, 8:40, 0:128]
            if x:
                t = pltpu.roll(t, 8 * x, 1)
            h = (8 * x - 8) % 128
            lo = jnp.where((lane >= 8 * x) & (lane < 8 * x + 8), t, lo)
            hi = jnp.where((lane >= h) & (lane < h + 8), t, hi)
        zs0[q, 0] = lo
        zs0[q, 1] = hi

    def pack1(q):
        lane = iota((16, 128), 1)
        out = jnp.zeros((16, 128), F32)
        for x in range(8):
            t = f1[q, 4 + x, 8:24, :]
            lo = t if x == 0 else pltpu.roll(t, 16 * x, 1)
            hi = t if x == 3 else pltpu.roll(t, (16 * x - 48) % 128, 1)
            out = jnp.where((lane >= 16 * x) & (lane < 16 * x + 8), lo, out)
            out = jnp.where((lane >= 16 * x + 8) & (lane < 16 * x + 16), hi, out)
        zs1[q] = out

    rho_in.wait()
    f1[0, 4:12, 8:24, 0:64] = rho[...]
    pack1(0)

    pl.semaphore_wait(barrier, len(reached))

    def rcopy(src, dst, k, d):
        return pltpu.make_async_remote_copy(
            src_ref=src, dst_ref=dst, send_sem=ss.at[k], recv_sem=rs.at[k], device_id=peer(d), device_id_type=MESH
        )

    def atom_copies():
        return [
            rcopy(at.at[0:16], at.at[16 * k + 16 : 16 * k + 32], k, d) for k, d in enumerate(UP7)
        ]

    def frame_slices(d, nx, hx, ny, part):
        near, far = part
        src, dst = [], []
        for s, n, h, o, a, b in ((d[0], nx, hx, hx, near, far), (d[1], ny, 8, 8, 0, 8)):
            if s == 0:
                src.append(slice(o, o + n))
                dst.append(slice(o, o + n))
            elif s > 0:
                src.append(slice(o + n - b, o + n - a))
                dst.append(slice(h - b, h - a))
            else:
                src.append(slice(o + a, o + b))
                dst.append(slice(o + n + a, o + n + b))
        return tuple(src), tuple(dst)

    def copies0(frame, q, base, part):
        out = []
        for k, d in enumerate(DIRS):
            src, dst = frame_slices(d, 16, 6, 32, part)
            if d[2] == 0:
                out.append(rcopy(frame.at[src + (slice(0, 128),)], frame.at[dst + (slice(0, 128),)], base + k, d))
            else:
                rows = slice(src[1].start - 8, src[1].stop - 8)
                zr = zh0 if d[2] > 0 else zl0
                out.append(rcopy(zs0.at[q, 1 if d[2] > 0 else 0, rows], zr.at[q, 1 - d[0], dst[1]], base + k, d))
        return out

    def late_copies():
        out = []
        for k, d in enumerate(XY_DIRS):
            src, dst = frame_slices(d, 16, 6, 32, (3, 5))
            out.append(rcopy(ff.at[src + (slice(0, 128),)], ff.at[dst + (slice(0, 128),)], SEM_LATE + k, d))
        return out

    def copies1(q, base, part):
        out = []
        for k, d in enumerate(DIRS):
            src, dst = frame_slices(d, 8, 4, 16, part)
            if d[2] == 0:
                out.append(rcopy(f1.at[(q,) + src], f1.at[(q,) + dst], base + k, d))
            else:
                rows = slice(src[1].start - 8, src[1].stop - 8)
                zr = zh1 if d[2] > 0 else zl1
                out.append(rcopy(zs1.at[q, rows], zr.at[q, 1 - d[0], dst[1]], base + k, d))
        return out

    def copies2(q, base):
        mine = t2.at[q, 1, 1, 8:16]
        return [
            rcopy(mine, t2.at[q, 1 - d[2], 1 - d[0], 8 * (1 - d[1]) : 8 * (1 - d[1]) + 8], base + k, d)
            for k, d in enumerate(DIRS)
        ]

    def copies3a(q, base):
        return [rcopy(x1.at[q, 0], x1.at[q, k + 1], base + k, (n, 0, 0)) for k, n in enumerate(X_NEAR)]

    def copies3b(q, base):
        return [
            rcopy(y1.at[q, 1, 8:16], y1.at[q, 1 - d[2], 8 * (1 - d[1]) : 8 * (1 - d[1]) + 8], base + k, d)
            for k, d in enumerate(YZ_NEAR)
        ]

    def copies4a(q, base):
        return [rcopy(xa.at[q, gx], xa.at[q, gx], base + k, (n, 0, 0)) for k, n in enumerate(RING)]

    def copies4b(q, base):
        return [rcopy(yb.at[q, gy], yb.at[q, gy], base + k, (0, n, 0)) for k, n in enumerate(RING)]

    def start(copies):
        for item in copies:
            item.start()

    def wait_recv(copies):
        for item in copies:
            item.wait_recv()

    def wait_send(copies):
        for item in copies:
            item.wait_send()

    def in_x(i):
        x = 16 * gx + i - 6
        return jnp.where((x >= 0) & (x < 128), 1.0, 0.0)

    def unpack0(frame, q, halo, own):
        lane = iota((48, 128), 1)
        keep = (lane < 8) | (lane >= 120)

        def beside(slot, sx, i):
            t = jnp.where((lane >= 8 * sx) & (lane < 8 * sx + 8), zl0[q, slot], zh0[q, slot])
            t = pltpu.roll(t, lax.rem(128 - 8 * sx, 128), 1)
            return jnp.where(keep, t, 0.0) * (k0[:, 128:256] * in_x(i))

        for i in halo:
            below = i < 6
            frame[i, :, 0:128] = frame[i, :, 0:128] * (k0[:, 0:128] * in_x(i))
            frame[i, :, 128:256] = beside(0 if below else 2, jnp.int32(i + 10 if below else i - 22), i)

        def body(k, carry):
            values = [(i, beside(1, i - 6, i)) for i in [4 * k + 6 + j for j in range(4)]]
            for i, value in values:
                frame[i, :, 128:256] = value
                for rows in (slice(0, 8), slice(40, 48)):
                    frame[i, rows, 0:128] = frame[i, rows, 0:128] * k0[rows, 0:128]
            return carry

        if own:
            lax.fori_loop(0, 4, body, 0)

    def unpack1(q):
        lane = iota((32, 128), 1)
        for i in range(16) if not isinstance(q, int) else range(3, 13):
            slot = 0 if i < 4 else 1 if i < 12 else 2
            sx = (4 + i) % 8 if i < 4 else (i - 4) % 8
            lo = zl1[q, slot]
            hi = zh1[q, slot]
            if (64 - 16 * sx) % 128:
                lo = pltpu.roll(lo, (64 - 16 * sx) % 128, 1)
            if (112 - 16 * sx) % 128:
                hi = pltpu.roll(hi, (112 - 16 * sx) % 128, 1)
            t = jnp.where(lane < 64, f1[q, i], jnp.where(lane < 72, lo, jnp.where(lane >= 120, hi, 0.0)))
            f1[q, i] = t * k1[i]

    def unpack2(q):
        lane = iota((24, 128), 1)
        for i in range(12):
            slot, sx = i // 4, i % 4
            below, mid, above = t2[q, 0, slot], t2[q, 1, slot], t2[q, 2, slot]
            if sx:
                mid = pltpu.roll(mid, 128 - 32 * sx, 1)
            if sx != 1:
                above = pltpu.roll(above, (32 - 32 * sx) % 128, 1)
            if sx != 3:
                below = pltpu.roll(below, 96 - 32 * sx, 1)
            t = jnp.where(lane < 32, mid, jnp.where(lane < 64, above, jnp.where(lane >= 96, below, 0.0)))
            f2[i] = t * k2[i]

    def unpack3(q):
        lane = iota((24, 128), 1)
        for dx in range(-2, 3):
            shift = 16 * lax.rem(gx + (dx + 8), 8)

            def turned(slot, target):
                return pltpu.roll(y1[q, slot], lax.rem(128 + target - shift, 128), 1)

            t = jnp.where(lane < 16, turned(1, 0), 0.0)
            t = jnp.where((lane >= 16) & (lane < 32), turned(2, 16), t)
            t = jnp.where(lane >= 112, turned(0, 112), t)
            for y in range(3):
                for x in range(2):
                    f3[2 * dx + 4 + x, 4 + 4 * y : 8 + 4 * y, :] = t[8 * y + 4 * x : 8 * y + 4 * x + 4]
        f3[...] = f3[...] * k3[...]

    def unpack4(q):
        lane = iota((64, 128), 1)
        for y in range(2):
            t = pltpu.roll(yb[q].reshape(64, 128), 120 - 32 * y, 1)
            ts[y] = jnp.where((lane < 16) | (lane >= 120), t, 0.0)
        for x in range(8):
            for y in range(2):
                f4[x, pl.ds(8 + y, 8, 2), :] = ts[y, pl.ds(x, 8, 8), :]

    def prolong0(source, first, add):
        es0[...] = mm(source.reshape(512, 128), prolong_matrix(128, 96, 256, 192)).reshape(16, 32, 256)

        def rows(k, carry):
            values = []
            for i in (first + 2 * k, first + 2 * k + 1):
                mid = 0.75 * es0[i, 4:28, :]
                even = (mid + 0.25 * es0[i, 3:27, :]) * ke[...]
                odd = (mid + 0.25 * es0[i, 5:29, :]) * ko[...]
                values.append((i, even, odd))
            for i, even, odd in values:
                ye0[i] = even
                yo0[i] = odd
            return carry

        lax.fori_loop(0, 8 - first, rows, 0)

        def planes(step, carry):
            for k in (first + 2 * step, first + 2 * step + 1):
                for x, pair_of in enumerate(plane_pair(ye0, yo0, 1, k)):
                    i = 2 * k + x
                    for y, value in enumerate(pair_of):
                        value = value * in_x(i)
                        for h in range(2):
                            at_rows = (h, i, pl.ds(y, 24, 2))
                            part = value[:, 128 * h : 128 * h + 128]
                            v1[at_rows] = v1[at_rows] + part if add else part
            return carry

        lax.fori_loop(0, 7 - first, planes, 0)

    rho_copies = copies1(0, SEM_RHO, (0, 1))
    start(rho_copies)
    hi_prec = lax.Precision.HIGHEST
    m = iota((9, 128), 0)
    c = iota((9, 128), 1)
    one = jnp.where((c < 7) & (m == c), 1.0, 0.0)
    one = one + jnp.where((c == 7) & (m == 7), 1.0, 0.0) - jnp.where((c == 7) & (m == 8), 1.0, 0.0)
    one = one - jnp.where((c == 8) & (m >= 7), 1.0, 0.0) + jnp.where((c == 9) & (m == 8), 2.0, 0.0)
    for item in small_in:
        item.wait()
    moments = lax.dot_general(
        pair[...], expn_t[...], (((1,), (1,)), ((), ())), precision=hi_prec, preferred_element_type=F32
    )
    packed = jnp.dot(moments, one, precision=hi_prec)
    corners = corner_t[...].astype(F32)
    tp[...] = jnp.zeros(tp.shape, F32)
    tp[10:13, 0:16] = corners + 5.5 + offset_t[...]
    tp[13:16, 0:16] = corners
    at[0:16, :] = packed + tp[...].T[0:16]
    atoms = atom_copies()
    start(atoms)
    v0_in.wait()
    pack0(vf, 0)
    v_copies = copies0(vf, 0, SEM_V, (0, 6))
    start(v_copies)

    for ref in (v1, g1, f3, e3, f4, v4, a2, w3):
        ref[...] = jnp.zeros(ref.shape, F32)
    k0[...] = grid_mask((1, 48, 256), (0, 32 * gy - 8, 128 * gz), (128, 256, 1024), 192, (-8, 136))[0]
    y_even = 2 * iota((24, 256), 0) + 32 * gy - 8
    z_at = wrapped(iota((24, 256), 1), 192, 256)
    z_in = (z_at >= -8) & (z_at < 136) & (z_at + 128 * gz >= 0) & (z_at + 128 * gz < 1024)
    y_in = (y_even >= 0) & (y_even < 256)
    ke[...] = jnp.where(y_in & z_in, 1.0, 0.0)
    ko[...] = ke[...]
    k1[...] = grid_mask((16, 32, 128), (8 * gx - 4, 16 * gy - 8, 64 * gz), (64, 128, 512), 96, (-8, 72))
    k2[...] = grid_mask((12, 24, 128), (4 * gx - 4, 8 * gy - 8, 32 * gz), (32, 64, 256), 96, (-32, 64))
    k3[...] = grid_mask((10, 24, 128), (2 * gx - 4, 4 * gy - 8, 16 * gz), (16, 32, 128), 64, (-16, 32))
    kg[...] = grid_mask((4, 16, 128), (2 * gx - 1, 4 * gy - 4, 16 * gz), (16, 32, 128), 64, (-16, 32))
    k4[...] = grid_mask((8, 32, 128), (0, -8, 8 * gz), (8, 16, 64), 64, (-8, 16))

    wait_send(rho_copies)
    wait_recv(rho_copies)
    unpack1(0)
    prolong0(f1[0], 3, False)

    wait_recv(atoms)
    by_atom = at[...]
    by_param = by_atom.T

    def factor(coord, centre, low):
        u = (coord - centre) * 0.5
        e = jnp.where((coord >= low) & (coord < low + 12.0), jnp.exp(-u * u), 0.0)
        return u, e

    def row(k):
        return by_param[k : k + 1, :]

    def coordinates(shape, dim, first):
        return (iota(shape, dim) + first).astype(F32)

    ux, ex = factor(coordinates((16, 128), 0, 16 * gx), row(10), row(13))
    uy, ey = factor(coordinates((32, 128), 0, 32 * gy), row(11), row(14))
    uz, ez = factor(coordinates((128, 128), 1, 128 * gz), by_atom[:, 12:13], by_atom[:, 15:16])
    uex = ux * ex
    p00 = row(0) * ex + row(1) * uex + row(7) * (ux * uex)
    p01 = row(2) * ex + row(4) * uex
    p02 = row(8) * ex
    p10 = row(3) * ex + row(6) * uex
    p11 = row(5) * ex
    p20 = row(9) * ex
    uey = uy * ey
    uuey = uy * uey
    for x in range(16):
        s = slice(x, x + 1)
        pln[32 * x : 32 * x + 32, 0:128] = p00[s] * ey + p01[s] * uey + p02[s] * uuey
        pln[32 * x : 32 * x + 32, 128:256] = p10[s] * ey + p11[s] * uey
        pln[32 * x : 32 * x + 32, 256:384] = p20[s] * ey
    uez = uz * ez
    z_hi, z_lo = split(jnp.concatenate([ez, uez, uz * uez], axis=0))
    p_hi, p_lo = split(pln[...])
    block = dot(p_hi, z_hi) + dot(p_hi, z_lo) + dot(p_lo, z_hi)
    gauss[...] = block.reshape(16, 32, 128)
    smooth[...] = v1[0, 6:22, 8:40, :]
    ff[6:22, 8:40, 0:128] = smooth[...] + gauss[...]
    parts_out = [
        pltpu.make_async_copy(smooth, smooth_out, local.at[6]),
        pltpu.make_async_copy(gauss, local_out, local.at[7]),
    ]

    pack0(ff, 1)
    f_copies = copies0(ff, 1, SEM_F, (0, 3))
    start(f_copies)
    late = late_copies()
    start(late)
    start(parts_out)
    wait_send(v_copies)
    wait_recv(v_copies)
    unpack0(vf, 0, (*range(6), *range(22, 28)), True)
    wait_recv(f_copies)
    unpack0(ff, 1, (3, 4, 5, 22, 23, 24), True)

    def cycle(q, carry):
        base = SEM_CYCLE + q * PER_CYCLE
        c1 = copies1(q + 1, base, (0, 4))
        c2 = copies2(q, base + N_DIR)
        c4a = copies4a(q, base + 2 * N_DIR)
        c4b = copies4b(q, base + 2 * N_DIR + N_RING)
        c3a = copies3a(q, base + 2 * N_DIR + 2 * N_RING)
        c3b = copies3b(q, base + 2 * N_DIR + 2 * N_RING + len(X_NEAR))

        def pre(first, count):
            values = []
            for i in [first + j for j in range(count)]:
                c = vf[i]
                value = 0.2 * c + ALPHA * (ff[i] + spread(c, vf[i - 1], vf[i + 1]))
                values.append((i, value * (k0[...] * in_x(i))))
            for i, value in values:
                v1[0, i] = value[:, 0:128]
                v1[1, i] = value[:, 128:256]

        @pl.loop(0, 2)
        def _(k):
            pre(11 * k + 3, 11)

        @pl.loop(0, 5)
        def _(k):
            sums = []
            for pair_at in (2 * k, 2 * k + 1):
                total = None
                for i in (2 * pair_at + 4, 2 * pair_at + 5):
                    c = both(v1, i)
                    r = ff[i] - 6.0 * c + spread(c, both(v1, i - 1), both(v1, i + 1))
                    total = r if total is None else total + r
                sums.append((pair_at, total))
            for n, (_, total) in enumerate(sums):
                s0[n, 0] = total[:, 0:128]
                s0[n, 1] = total[:, 128:256]
            for n, (pair_at, _) in enumerate(sums):
                a0[pair_at] = jnp.concatenate([halve_rows(s0.at[n, h], 0, 24) for h in range(2)], axis=1)

        g = 0.125 * mm(a0[...].reshape(240, 256), restrict_matrix(256, 192, 128, 96))
        g1[:, 4:28, :] = g.reshape(10, 24, 128)
        g1[...] = g1[...] * k1[3:13]
        f1[q + 1, 4:12, 8:24, :] = g1[1:9, 8:24, :]

        c, nb = neighbours(g1, 1, 8)
        r = (0.2 * c + ALPHA * nb).reshape(4, 2, 32, 128)
        s1[...] = r[:, 0] + r[:, 1]
        parts = jnp.concatenate(
            [s1[x, pl.ds(8, 8, 2), :] + s1[x, pl.ds(9, 8, 2), :] for x in range(4)], axis=1
        )
        row_at = iota((512, 128), 0)
        col_at = iota((512, 128), 1)
        lane_at = row_at & 127
        m2 = jnp.where((lane_at < 64) & ((row_at >> 7) * 32 + (lane_at >> 1) == col_at), 1.0, 0.0).astype(BF16)
        t2[q, 1, 1, 8:16] = 0.125 * mm(parts, m2)
        start(c2)
        pack1(q + 1)

        wait_recv(c2)
        unpack2(q)
        c, nb = neighbours(f2, 2, 8)
        r = (0.2 * c + ALPHA * nb).reshape(4, 2, 24, 128)
        s2[...] = r[:, 0] + r[:, 1]
        a2[:, 0:12, :] = s2[:, pl.ds(0, 12, 2), :] + s2[:, pl.ds(1, 12, 2), :]
        g = 0.125 * mm(a2[...].reshape(64, 128), restrict_matrix(128, 96, 128, 64))
        g3[...] = g.reshape(4, 16, 128) * kg[...]
        c, nb = neighbours(g3, 1, 2)
        r = 0.2 * c + ALPHA * nb
        s4[...] = r[0] + r[1]
        parts = jnp.concatenate([s4[4:5] + s4[5:6], s4[6:7] + s4[7:8]], axis=1)
        row_at = iota((256, 128), 0)
        z_at = wrapped(row_at & 127, 64, 128) >> 1
        live = (z_at >= -8) & (z_at < 16) & (z_at + 8 * gz >= 0) & (z_at + 8 * gz < 64)
        m4 = jnp.where(live & (32 * (row_at >> 7) + z_at + 8 == iota((256, 128), 1)), 1.0, 0.0).astype(BF16)
        xa[q, gx] = 0.125 * mm(jnp.broadcast_to(parts, (8, 256)), m4)[0:1]
        start(c4a)
        tile = jnp.concatenate([g3[1, 4:8, :], g3[2, 4:8, :]], axis=0)
        x1[q, 0] = pltpu.roll(jnp.where(iota((8, 128), 1) < 16, tile, 0.0), 16 * gx, 1)
        start(c3a)
        start(c1)
        wait_send(c2)
        wait_recv(c4a)
        yb[q, gy] = xa[q].reshape(8, 128)
        start(c4b)
        wait_recv(c3a)
        total = x1[q, 0]
        for n in range(len(X_NEAR)):
            total = total + x1[q, n + 1]
        y1[q, 1, 8:16] = total
        start(c3b)
        wait_send(c4a)
        wait_send(c3a)

        @pl.when(q == 0)
        def _():
            wait_send(f_copies)
            wait_send(late)
            wait_recv(late)
            unpack0(ff, 1, (1, 2, 25, 26), False)
            pre(1, 2)
            pre(25, 2)

        wait_send(c1)
        wait_recv(c1)
        unpack1(q + 1)
        wait_recv(c3b)
        unpack3(q)
        wait_recv(c4b)
        unpack4(q)

        weight4, weight3, weight2, weight1 = (ALPHA * 4.0**level for level in (4, 3, 2, 1))
        v4[4:12] = weight4 * f4[...]
        for _ in range(3):
            c, nb = neighbours(v4, 4, 8)
            v4[4:12] = (0.2 * c + ALPHA * nb + weight4 * f4[...]) * k4[...]

        near = v4[pl.ds(gx + 1, 7)].reshape(224, 128)
        es3[...] = mm(near, prolong_matrix(128, 64, 128, 64)).reshape(7, 32, 128)
        expand_rows(es3, ye3, yo3, 2 * gy + 4, 12)
        for k in range(5):
            expand_planes(ye3, yo3, w3, 0, 1, k)
        rhs = weight3 * f3[...]
        e3[...] = (rhs + w3[...]) * k3[...]
        c, nb = neighbours(e3, 1, 8)
        e3[1:9] = (0.2 * c + ALPHA * nb + rhs[1:9]) * k3[1:9]

        near = e3[1:9].reshape(192, 128)
        es2[...] = mm(near, prolong_matrix(128, 64, 128, 96)).reshape(8, 24, 128)
        expand_rows(es2, ye2, yo2, 4, 12)
        for k in range(6):
            expand_planes(ye2, yo2, w2, 0, 1, k)
        rhs = weight2 * f2[...]
        e2[...] = (rhs + w2[...]) * k2[...]
        c, nb = neighbours(e2, 1, 10)
        e2[1:11] = (0.2 * c + ALPHA * nb + rhs[1:11]) * k2[1:11]

        es1[...] = mm(e2[...].reshape(288, 128), prolong_matrix(128, 96, 128, 96)).reshape(12, 24, 128)
        expand_rows(es1, ye1, yo1, 4, 16)
        for k in range(8):
            expand_planes(ye1, yo1, w1, 0, 2, k)
        rhs = weight1 * f1[q + 1]
        e1[...] = (rhs + w1[...]) * k1[...]
        c, nb = neighbours(e1, 1, 14)
        e1[1:15] = (0.2 * c + ALPHA * nb + rhs[1:15]) * k1[1:15]

        prolong0(e1[...], 2 * q, True)

        source = jnp.where(q == 0, 1.0, 0.0)

        def post(k, carry):
            values = []
            for i in [8 * k + 4 * q + 2 + j for j in range(8)]:
                c = both(v1, i)
                value = 0.2 * c + ALPHA * (source * ff[i] + spread(c, both(v1, i - 1), both(v1, i + 1)))
                values.append((i, value * (k0[...] * in_x(i))))
            for i, value in values:
                vf[i] = value
            return carry

        lax.fori_loop(0, 3 - q, post, 0)
        wait_send(c4b)
        wait_send(c3b)
        return carry

    lax.fori_loop(0, 2, cycle, 0)
    result = pltpu.make_async_copy(vf.at[6:22, 8:40, 0:128], sweep_out, local.at[8])
    result.start()
    wait_send(atoms)
    for item in parts_out:
        item.wait()
    result.wait()


def scratch():
    def vm(*shape):
        return pltpu.VMEM(shape, F32)

    return [
        vm(16, 32, 128), vm(16, 32, 128), vm(16, 91), vm(9, 91), pltpu.VMEM((3, 16), jnp.int32), vm(3, 16),
        vm(28, 48, 256), vm(2, 28, 48, 128), vm(28, 48, 256),
        vm(2, 3, 48, 128), vm(2, 3, 48, 128), vm(2, 2, 32, 128), vm(8, 16, 64),
        vm(3, 16, 32, 128), vm(3, 3, 32, 128), vm(3, 3, 32, 128), vm(3, 16, 128),
        vm(10, 32, 128), vm(10, 24, 256), vm(2, 2, 48, 128), vm(16, 32, 256), vm(16, 24, 256), vm(16, 24, 256),
        vm(16, 32, 128), vm(16, 32, 128), vm(12, 24, 128), vm(12, 16, 128), vm(12, 16, 128),
        vm(2, 3, 3, 24, 128), vm(12, 24, 128), vm(12, 24, 128), vm(12, 24, 128), vm(4, 32, 128),
        vm(8, 24, 128), vm(8, 12, 128), vm(8, 12, 128),
        vm(2, 5, 8, 128), vm(2, 3, 24, 128), vm(10, 24, 128), vm(10, 24, 128), vm(10, 24, 128),
        vm(4, 24, 128), vm(4, 16, 128), vm(4, 16, 128), vm(16, 128), vm(7, 32, 128), vm(7, 12, 128), vm(7, 12, 128),
        vm(2, 8, 1, 128), vm(2, 8, 8, 128), vm(2, 64, 128), vm(8, 32, 128), vm(16, 32, 128),
        vm(128, 128), vm(128, 128), vm(512, 384),
        vm(48, 256), vm(24, 256), vm(24, 256),
        vm(16, 32, 128), vm(12, 24, 128), vm(10, 24, 128), vm(4, 16, 128), vm(8, 32, 128),
        pltpu.SemaphoreType.DMA((9,)), pltpu.SemaphoreType.DMA((N_SEMS,)), pltpu.SemaphoreType.DMA((N_SEMS,)),
    ]


def per_device(coarse_density, start_potential, pair_density, expansion, box_corners, box_offsets, lists, counts):
    del lists, counts
    block = jax.ShapeDtypeStruct((16, 32, 128), F32)
    hbm = pl.BlockSpec(memory_space=pltpu.HBM)
    smooth, gauss, sweep = pl.pallas_call(
        kernel,
        out_shape=(block, block, block),
        in_specs=[hbm] * 6,
        out_specs=(hbm, hbm, hbm),
        scratch_shapes=scratch(),
        compiler_params=pltpu.CompilerParams(
            collective_id=0, has_side_effects=True, vmem_limit_bytes=64 * 2**20
        ),
    )(coarse_density, start_potential, pair_density, expansion.T, box_corners.T, box_offsets.T)
    total_density = smooth + gauss
    return total_density, sweep + ALPHA * total_density


def solution(mesh):
    everywhere = P(AXES, None)
    in_specs = (P(*AXES), P(*AXES), everywhere, P(), everywhere, everywhere, everywhere, P(AXES))
    return jax.shard_map(
        per_device, mesh=mesh, in_specs=in_specs, out_specs=(P(*AXES), P(*AXES)), check_vma=False
    )
```
